256 devices in a mesh: dp: 8 (over y, core), label: 32 (over x, z).
Axes of the slice: x: 4, y: 4, z: 8, core: 2. Of those that a mesh axis runs over, the one named last changes fastest.
Arguments:
- encoded: bfloat16 [32768, 1024], P(('dp', 'label')), may hold values from -6 to 6
- positive_clusters: int32 [32768, 4], P(('dp', 'label')), may hold values from 0 to 16383
- cluster_weight: bfloat16 [16384, 1024], P('label'), may hold values from -0.1875 to 0.1875
- shortlist: int32 [32768, 4], P(('dp', 'label')), may hold values from 0 to 511, all different within a row; in each aligned block of 128 rows (0 to 127, 128 to 255, ...) at most 2 rows name the same one
- positive_offsets: int32 [32768, 4], P(('dp', 'label')), may hold values from 0 to 127
- block_weight: bfloat16 [512, 128, 1024], P('label'), may hold values from -0.1875 to 0.1875
Outputs:
- grad_hidden: bfloat16 [32768, 1024], P(('dp', 'label'))
- grad_cluster: float32 [16384, 1024], P('label', 'dp')
- grad_block: float32 [512, 128, 1024], P('label', None, 'dp')
The draws below stay inside these ranges and needn't reach their ends.
Inputs may be any that keep to these rules, and one draw needn't show every extreme that they name: `shortlist`: each row names 4 different blocks. Among the rows of one device no block is named more than 2 times, and in every draw some block is named exactly 2 times by the rows of some device.
All inputs are finite; a program needn't handle non-finite values.
Results may differ from the reference program's by a relative error of at most 0.018.
Values may be sent and summed in bfloat16 or wider, within the bound.
A program may use at most 128 MiB of HBM per device.

```python
import math
import jax
import jax.numpy as jnp
import numpy as np
from jax import lax

D = 1024
C1_DEV = 512
LBL = 128
K = 4
P1 = 4
DOC_DEV = 128
DOCS = 32768
C1 = 16384
NBLK = 512
CAP = 2
N_DP = 8
N_LABEL = 32


def touch_ends(array, rng, low, top_value):
    index_at = [jax.random.randint(jax.random.fold_in(rng, axis), (), 0, length) for axis, length in enumerate(array.shape)]
    widest = array.shape.index(max(array.shape))
    next_to = index_at[:widest] + [(index_at[widest] + 1) % array.shape[widest]] + index_at[widest + 1:]
    return array.at[tuple(index_at)].set(low).at[tuple(next_to)].set(top_value)


def block_levels(own_key, extent, pieces, least, top_value):
    gain = 1.0
    for position, blocks in pieces:
        heights = jax.random.uniform(jax.random.fold_in(jax.random.fold_in(own_key, 6), position), (blocks,), jnp.float32, least / len(pieces), top_value / len(pieces))
        gain = gain * jnp.repeat(jnp.exp(heights), extent[position] // blocks).reshape((-1,) + (1,) * (len(extent) - 1 - position))
    return gain


def deal_out(key, own, number, rows, amount, top, bound, lean):
    ranking = jax.random.permutation(key, amount)
    packed, ordinary = portions_of(amount, rows * top, bound, lean, True), portions_of(amount, rows * top, bound, lean, False)
    places = jnp.arange(amount)

    def named(tallies, rotation):
        used = int((tallies > 0).sum())
        fixed = max(1, used // 4)
        passed = fixed + (places - fixed + rotation * (used - fixed)) % max(1, amount - fixed)
        return jnp.zeros((amount,), jnp.int32).at[ranking[jnp.where(places < fixed, places, passed)]].set(jnp.asarray(tallies, jnp.int32))

    tallies = jnp.where(number % 4 == 0, named(packed, number // 4), named(ordinary, number - number // 4 - 1))
    mixed = jax.random.permutation(jax.random.fold_in(own, 3), amount)
    giver, sink = mixed[0:amount // 2 * 2:2], mixed[1:amount // 2 * 2:2]
    slack = jnp.minimum(tallies[giver] - 1, bound - tallies[sink]) // 2
    slack = jnp.where((giver == ranking[0]) | (sink == ranking[0]) | (tallies[sink] == 0), 0, jnp.maximum(slack, 0))
    passed = jax.random.randint(jax.random.fold_in(own, 4), (amount // 2,), 0, 1 << 20) % (slack + 1)
    tallies = tallies.at[giver].add(-passed).at[sink].add(passed)
    members = jnp.searchsorted(jnp.cumsum(tallies), jnp.arange(rows * top), side="right").astype(jnp.int32)
    grid = members.reshape(top, rows).T
    grid = grid[jax.random.permutation(jax.random.fold_in(own, 1), rows)]
    rotation = jax.random.randint(jax.random.fold_in(own, 2), (rows, 1), 0, top)
    return jnp.take_along_axis(grid, (jnp.arange(top)[None, :] + rotation) % top, axis=1)


def portions_of(count, total, limit, slope, full):
    loads = [(1 << 20) // math.isqrt(grade ** slope) + 1 for grade in range(1, count + 1)]
    largest = limit if full else min(limit, max(-(-total // count), total * loads[0] // sum(loads)))
    least = 1 if total - largest >= count - 1 else 0
    given, surplus = [largest] + [least] * (count - 1), total - largest - least * (count - 1)
    while surplus > 0:
        free = [i for i in range(1, count) if given[i] < largest] or [i for i in range(1, count) if given[i] < limit]
        mass, left = sum([loads[i] for i in free]), surplus
        for i in free:
            addition = min(limit - given[i], max(1, left * loads[i] // mass), surplus)
            given[i] = given[i] + addition
            surplus = surplus - addition
    return np.array(given)


def centred(own_key, extent, width, most, cuts=(), kind=jnp.bfloat16):
    array = jax.random.normal(own_key, extent, jnp.float32) * width
    if len(cuts) > 0:
        array = block_levels(own_key, extent, cuts, -0.22, 0.18) * array
    return jnp.clip(array, min=-most, max=most).astype(kind)


def setup_inputs(seed: int = 0) -> dict:
    streams_of = jax.random.split(jax.random.key(seed), 7)
    encoded = centred(streams_of[0], (DOCS, D), 1.0, 6.0, ((0, 256),))
    positive_clusters = touch_ends(jax.random.randint(streams_of[1], (DOCS, P1), 0, C1), jax.random.fold_in(streams_of[1], 1), 0, C1 - 1).astype(jnp.int32)
    cluster_weight = centred(streams_of[2], (C1, D), D ** -0.5, 0.1875, ((0, 32),))
    shortlist_keys = jax.random.split(jax.random.fold_in(streams_of[3], 1), DOCS // DOC_DEV)
    shortlist_turns = jax.random.permutation(jax.random.fold_in(streams_of[3], 3), DOCS // DOC_DEV)
    shortlist = jax.vmap(lambda own, number: deal_out(jax.random.fold_in(streams_of[3], 2), own, number, DOC_DEV, NBLK, K, CAP, 2))(shortlist_keys, shortlist_turns).reshape((DOCS, K))
    positive_offsets = touch_ends(jax.random.randint(streams_of[4], (DOCS, K), 0, LBL), jax.random.fold_in(streams_of[4], 1), 0, LBL - 1).astype(jnp.int32)
    block_weight = centred(streams_of[5], (NBLK, LBL, D), D ** -0.5, 0.1875, ((0, 32),))
    return {"encoded": encoded, "positive_clusters": positive_clusters, "cluster_weight": cluster_weight, "shortlist": shortlist, "positive_offsets": positive_offsets, "block_weight": block_weight}


def reference(encoded, positive_clusters, cluster_weight, shortlist, positive_offsets, block_weight):
    shards = cluster_weight.reshape(N_LABEL, C1_DEV, D)
    firsts = (jnp.arange(N_LABEL, dtype=jnp.int32) * C1_DEV).astype(jnp.int32)

    def level_one(total, inputs):
        weight, first = inputs
        scores = jnp.dot(encoded, weight.T, preferred_element_type=jnp.float32)
        ids = first + jnp.arange(C1_DEV, dtype=jnp.int32)
        hits = jnp.zeros(scores.shape, dtype=bool)
        for column in range(P1):
            hits = hits | (positive_clusters[:, column:column + 1] == ids[None, :])
        delta = (jax.nn.sigmoid(scores) - hits.astype(jnp.float32)).astype(jnp.bfloat16)
        part = jnp.dot(delta, weight, preferred_element_type=jnp.float32).astype(jnp.bfloat16)
        part = lax.optimization_barrier(part)
        grad = jnp.dot(delta.T, encoded, preferred_element_type=jnp.float32)
        return (total + part.astype(jnp.float32), grad)
    hidden_one, grads = lax.scan(level_one, jnp.zeros((DOCS, D), jnp.float32), (shards, firsts))
    scale = 1.0 / jnp.sqrt(jnp.float32(DOCS))
    grad_cluster = grads.reshape(C1, D) * scale
    pairs = DOCS * K
    flat_block = shortlist.reshape(-1).astype(jnp.int32)
    flat_doc = (jnp.arange(pairs, dtype=jnp.int32) // K).astype(jnp.int32)
    flat_off = positive_offsets.reshape(-1).astype(jnp.int32)
    order = jnp.argsort(flat_block, stable=True).astype(jnp.int32)
    sorted_block = flat_block[order]
    counts = jnp.zeros((NBLK,), jnp.int32).at[flat_block].add(1)
    starts = (jnp.cumsum(counts) - counts).astype(jnp.int32)
    place = (jnp.arange(pairs, dtype=jnp.int32) - starts[sorted_block]).astype(jnp.int32)
    most_rows = CAP * N_DP * N_LABEL
    table = jnp.full((NBLK, most_rows), -1, jnp.int32).at[sorted_block, place].set(order)
    label_ids = jnp.arange(LBL, dtype=jnp.int32)

    def level_two(total, inputs):
        row, weight = inputs
        valid = row >= 0
        index = jnp.where(valid, row, 0).astype(jnp.int32)
        docs = flat_doc[index]
        rows = encoded[docs]
        scores = jnp.dot(rows, weight.T, preferred_element_type=jnp.float32)
        target = (flat_off[index][:, None] == label_ids[None, :]).astype(jnp.float32)
        delta = jnp.where(valid[:, None], jax.nn.sigmoid(scores) - target, 0.0).astype(jnp.bfloat16)
        back = jnp.dot(delta, weight, preferred_element_type=jnp.float32).astype(jnp.bfloat16)
        back = lax.optimization_barrier(back)
        added = jnp.where(valid[:, None], back.astype(jnp.float32), 0.0)
        total = total.at[docs].add(added)
        grad = jnp.dot(delta.T, rows, preferred_element_type=jnp.float32)
        return (total, grad)
    hidden_two, block_grads = lax.scan(level_two, jnp.zeros((DOCS, D), jnp.float32), (table, block_weight))
    grad_block = block_grads * scale
    grad_hidden = (hidden_one + hidden_two).astype(jnp.bfloat16)
    return (grad_hidden, grad_cluster, grad_block)
```

```python
import math

import jax
import jax.numpy as jnp
from jax import lax
from jax.experimental import pallas as pl
from jax.experimental.pallas import tpu as pltpu
from jax.sharding import PartitionSpec as P

MESH = pl.DeviceIdType.MESH
F32, BF16 = jnp.float32, jnp.bfloat16
NY, NC, NX, NZ = 4, 2, 4, 8
DOC, D, CL, LBL = 128, 1024, 512, 128
VMEM_LIMIT = 60 * 1024 * 1024


class Spot:
    def __init__(self):
        dp, label = lax.axis_index("dp"), lax.axis_index("label")
        self.y, self.c = dp // NC, dp % NC
        self.x, self.z = label // NZ, label % NZ

    def at(self, dx=0, dy=0, dz=0, dc=0):
        y, x, z = (self.y + dy) % NY, (self.x + dx) % NX, (self.z + dz) % NZ
        return (y * NC + (self.c + dc) % NC, x * NZ + z)


def greet(others):
    barrier = pltpu.get_barrier_semaphore()
    for other in others:
        pl.semaphore_signal(barrier, inc=1, device_id=other, device_id_type=MESH)
    pl.semaphore_wait(barrier, len(others))


class Copies:
    def __init__(self, send, recv):
        self.send, self.recv, self.used, self.sent = send, recv, 0, []

    def start(self, src, dst, device):
        i = self.used
        self.used += 1
        copy = pltpu.make_async_remote_copy(
            src_ref=src, dst_ref=dst, send_sem=self.send.at[i], recv_sem=self.recv.at[i],
            device_id=device, device_id_type=MESH,
        )
        copy.start()
        self.sent.append(copy)
        return copy

    def finish(self):
        for copy in self.sent:
            copy.wait_send()


def dot(a, b, dims):
    return lax.dot_general(a, b, (dims, ((), ())), preferred_element_type=F32)


def gather_kernel(enc, w, meta, docs, wrel, metas, arr, tgt, place, disp, send, recv, local):
    me = Spot()
    x, y, z, c = me.x, me.y, me.z, me.c
    greet(
        [me.at(dz=i) for i in range(1, NZ)] + [me.at(dx=i) for i in range(1, NX)]
        + [me.at(dy=1), me.at(dy=-1), me.at(dc=1)]
    )
    cp = Copies(send, recv)
    half = DOC // 2
    right = cp.start(enc, docs.at[z], me.at(dz=1))
    left = cp.start(enc, docs.at[z], me.at(dz=-1))
    got_meta = [None] + [cp.start(meta, metas.at[z], me.at(dz=i)) for i in range(1, NZ)]
    w_right = cp.start(w.at[y, c], wrel.at[3, y, c], me.at(dx=1))
    w_left = cp.start(w.at[y, c], wrel.at[1, y, c], me.at(dx=-1))
    own = [
        pltpu.make_async_copy(w, wrel.at[0], local.at[0]),
        pltpu.make_async_copy(enc, docs.at[z], local.at[1]),
        pltpu.make_async_copy(meta, metas.at[z], local.at[2]),
    ]
    for copy in own:
        copy.start()

    slot = lax.broadcasted_iota(jnp.int32, (128, 128), 0)
    block = (((x + (slot >> 5)) & 3) * NZ + z) * 16 + (slot & 15)
    turn = ((slot >> 4) & 1).astype(F32)
    lane = lax.broadcasted_iota(jnp.int32, (128, 128), 1)
    upper = jnp.where(slot < lane, 1.0, 0.0).astype(BF16)
    row8 = lax.broadcasted_iota(jnp.int32, (8, 128), 0)
    tgt[0] = jnp.zeros((8, 128), F32)
    arrivals = []

    def dispatch(zs):
        info = metas[zs]
        named = jnp.zeros((128, 128), F32)
        offset = jnp.zeros((128, 128), F32)
        for k in range(4):
            hit = info[4 + k:5 + k, :] == block
            named = jnp.where(hit, 1.0, named)
            offset = jnp.where(hit, (info[8 + k:9 + k, :] + 1).astype(F32), offset)
        rank = dot(named.astype(BF16), upper, ((1,), (0,)))
        chosen = jnp.where(rank == turn, named, 0.0)
        place[zs] = chosen.astype(BF16)
        disp[zs] = dot(chosen.astype(BF16), docs[zs], ((1,), (0,))).astype(BF16)
        pick = jnp.where(row8 == zs, 1.0, 0.0).astype(BF16)
        tgt[0] += dot(pick, (chosen * offset).astype(BF16), ((1,), (1,)))
        for d in range(1, NX):
            arrivals.append(
                cp.start(disp.at[zs, pl.ds(d * 32, 32)], arr.at[NX - d, zs], me.at(dx=d))
            )
        arr[0, zs] = disp[zs, 0:32]

    own[1].wait()
    own[2].wait()
    dispatch(z)
    groups = pl.ds(1, 3)
    for h in range(1, NZ // 2):
        from_left, from_right = (z - h) % NZ, (z + h) % NZ
        right.wait_recv()
        left.wait_recv()
        if h + 1 < NZ // 2:
            right = cp.start(docs.at[from_left], docs.at[from_left], me.at(dz=1))
            left = cp.start(docs.at[from_right], docs.at[from_right], me.at(dz=-1))
        else:
            right = cp.start(
                docs.at[from_left, pl.ds(0, half)], docs.at[from_left, pl.ds(0, half)], me.at(dz=1)
            )
            left = cp.start(
                docs.at[from_right, pl.ds(half, half)], docs.at[from_right, pl.ds(half, half)], me.at(dz=-1)
            )
        if h == 1:
            w_right.wait_recv()
            w_left.wait_recv()
            w_right = cp.start(w_part(wrel, 3, y, c, 0), w_part(wrel, 2, y, c, 0), me.at(dx=1))
            w_left = cp.start(w_part(wrel, 1, y, c, 1), w_part(wrel, 2, y, c, 1), me.at(dx=-1))
        if h == 2:
            w_right.wait_recv()
            w_left.wait_recv()
            y_right = cp.start(wrel.at[groups, y, c], wrel.at[groups, y, c], me.at(dy=1))
            y_left = cp.start(wrel.at[groups, y, c], wrel.at[groups, y, c], me.at(dy=-1))
            sib = [cp.start(wrel.at[groups, y, c], wrel.at[groups, y, c], me.at(dc=1))]
        if h == 3:
            y_right.wait_recv()
            y_left.wait_recv()
            yl, yr = (y - 1) % NY, (y + 1) % NY
            sib.append(cp.start(wrel.at[groups, yl, c], wrel.at[groups, yl, c], me.at(dc=1)))
            sib.append(cp.start(wrel.at[groups, yr, c], wrel.at[groups, yr, c], me.at(dc=1)))
            a, b = pl.ds(0, 32), pl.ds(32, 32)
            y_right = cp.start(wrel.at[groups, yl, c, a], wrel.at[groups, yl, c, a], me.at(dy=1))
            y_left = cp.start(wrel.at[groups, yr, c, b], wrel.at[groups, yr, c, b], me.at(dy=-1))
        got_meta[h].wait_recv()
        dispatch(from_left)
        got_meta[NZ - h].wait_recv()
        dispatch(from_right)
    y_right.wait_recv()
    y_left.wait_recv()
    far = (y + 2) % NY
    sib.append(cp.start(wrel.at[groups, far, c], wrel.at[groups, far, c], me.at(dc=1)))
    right.wait_recv()
    left.wait_recv()
    got_meta[NZ // 2].wait_recv()
    dispatch((z + NZ // 2) % NZ)
    for d in range(1, NX):
        arrivals.append(cp.start(tgt.at[0], tgt.at[NX - d], me.at(dx=d)))
    for copy in arrivals + sib:
        copy.wait_recv()
    own[0].wait()
    cp.finish()


def w_part(wrel, group, y, c, part):
    return wrel.at[group, y, c, pl.ds(part * 32, 32)]


def gather(enc, w, meta):
    vmem = pl.BlockSpec(memory_space=pltpu.VMEM)
    copies = 64
    return pl.pallas_call(
        gather_kernel,
        out_shape=(
            jax.ShapeDtypeStruct((NZ, DOC, D), BF16),
            jax.ShapeDtypeStruct((NX, NY, NC, 64, D), BF16),
            jax.ShapeDtypeStruct((NZ, 16, 128), jnp.int32),
            jax.ShapeDtypeStruct((NX, NZ, 32, D), BF16),
            jax.ShapeDtypeStruct((NX, NZ, 128), F32),
            jax.ShapeDtypeStruct((NZ, 128, 128), BF16),
        ),
        in_specs=[vmem] * 3,
        out_specs=(vmem,) * 6,
        scratch_shapes=[
            pltpu.VMEM((NZ, 128, D), BF16),
            pltpu.SemaphoreType.DMA((copies,)),
            pltpu.SemaphoreType.DMA((copies,)),
            pltpu.SemaphoreType.DMA((3,)),
        ],
        compiler_params=pltpu.CompilerParams(
            collective_id=0, has_side_effects=True, vmem_limit_bytes=VMEM_LIMIT
        ),
    )(enc, w.reshape(NY, NC, 64, D), meta)


def reduce_kernel(
    back, place, hidden, gc, gb, out_h, out_c, out_b,
    ret, hid, zs_r, zs_l, zr_r, zr_l,
    c_in, c_sum, x_r2, x_l2, x_s, x_r, x_y, cy_2, cy_s, cy_r,
    b_in, b_sum, by_2, by_s, by_r, send, recv,
):
    me = Spot()
    x, y, z, c = me.x, me.y, me.z, me.c
    greet(
        [me.at(dx=i) for i in range(1, NX)]
        + [me.at(dz=1), me.at(dz=-1), me.at(dy=1), me.at(dy=-1), me.at(dc=1)]
    )
    cp = Copies(send, recv)
    returns = [
        cp.start(back.at[e], ret.at[pl.ds(0, NZ), pl.ds((NX - e) * 32, 32)], me.at(dx=e)) for e in range(1, NX)
    ]
    b_core = cp.start(gb.at[pl.ds(0, NY), 1 - c], b_in, me.at(dc=1))
    c_core = cp.start(gc.at[pl.ds(0, NY), 1 - c], c_in, me.at(dc=1))
    for i in range(NZ):
        ret[i, 0:32] = back[0, i]

    b_core.wait_recv()

    def add_block(i, carry):
        rows = pl.ds(pl.multiple_of((i % 4) * 512, 512), 512)
        b_sum[i // 4, rows] = (gb[i // 4, c, rows].astype(F32) + b_in[i // 4, rows].astype(F32)).astype(BF16)
        return carry

    lax.fori_loop(0, 16, add_block, 0)
    top, low = pl.ds(0, 1024), pl.ds(1024, 1024)
    far = (y + 2) % NY
    b_right = cp.start(b_sum.at[far, top], by_2.at[top], me.at(dy=1))
    b_left = cp.start(b_sum.at[far, low], by_2.at[low], me.at(dy=-1))

    c_core.wait_recv()

    def add_cluster(i, carry):
        g, t = i // 4, i % 4
        c_sum[g, t] = (gc[t, c, g].astype(F32) + c_in[t, g].astype(F32)).astype(BF16)
        return carry

    lax.fori_loop(0, 16, add_cluster, 0)
    x_right = cp.start(c_sum.at[2, pl.ds(0, 2)], x_r2, me.at(dx=1))
    x_left = cp.start(c_sum.at[2, pl.ds(2, 2)], x_l2, me.at(dx=-1))

    for copy in returns:
        copy.wait_recv()

    def combine(t):
        hid[t] = hidden[t] + dot(place[t], ret[t], ((0,), (0,)))

    half = DOC // 2
    t = (z + 4) % NZ
    combine(t)
    zs_r[3, 0:half] = hid[t, 0:half].astype(BF16)
    zs_l[3, half:DOC] = hid[t, half:DOC].astype(BF16)
    a, b = pl.ds(0, half), pl.ds(half, half)
    z_right = cp.start(zs_r.at[3, a], zr_r.at[3, a], me.at(dz=1))
    z_left = cp.start(zs_l.at[3, b], zr_l.at[3, b], me.at(dz=-1))

    def z_step(h):
        right, left = (z + h) % NZ, (z - h) % NZ
        combine(right)
        combine(left)
        z_right.wait_recv()
        z_left.wait_recv()
        if h == 3:
            zs_r[2, 0:half] = (hid[right, 0:half] + zr_r[3, 0:half].astype(F32)).astype(BF16)
            zs_r[2, half:DOC] = hid[right, half:DOC].astype(BF16)
            zs_l[2, half:DOC] = (hid[left, half:DOC] + zr_l[3, half:DOC].astype(F32)).astype(BF16)
            zs_l[2, 0:half] = hid[left, 0:half].astype(BF16)
        else:
            zs_r[h - 1] = (hid[right] + zr_r[h].astype(F32)).astype(BF16)
            zs_l[h - 1] = (hid[left] + zr_l[h].astype(F32)).astype(BF16)
        return (
            cp.start(zs_r.at[h - 1], zr_r.at[h - 1], me.at(dz=1)),
            cp.start(zs_l.at[h - 1], zr_l.at[h - 1], me.at(dz=-1)),
        )

    z_right, z_left = z_step(3)

    x_right.wait_recv()
    x_left.wait_recv()

    def add_x(i, carry):
        x_s[0, i] = (c_sum[1, i].astype(F32) + x_r2[i].astype(F32)).astype(BF16)
        x_s[0, i + 2] = c_sum[1, i + 2]
        x_s[1, i + 2] = (c_sum[3, i + 2].astype(F32) + x_l2[i].astype(F32)).astype(BF16)
        x_s[1, i] = c_sum[3, i]
        return carry

    lax.fori_loop(0, 2, add_x, 0)
    x_right = cp.start(x_s.at[0], x_r.at[0], me.at(dx=1))
    x_left = cp.start(x_s.at[1], x_r.at[1], me.at(dx=-1))

    b_right.wait_recv()
    b_left.wait_recv()
    up, down = (y + 1) % NY, (y - 1) % NY

    def add_b(i, carry):
        rows = pl.ds(pl.multiple_of(i * 512, 512), 512)
        other = pl.ds(pl.multiple_of(i * 512 + 1024, 512), 512)
        by_s[0, rows] = (b_sum[up, rows].astype(F32) + by_2[rows].astype(F32)).astype(BF16)
        by_s[0, other] = b_sum[up, other]
        by_s[1, other] = (b_sum[down, other].astype(F32) + by_2[other].astype(F32)).astype(BF16)
        by_s[1, rows] = b_sum[down, rows]
        return carry

    lax.fori_loop(0, 2, add_b, 0)
    b_right = cp.start(by_s.at[0], by_r.at[0], me.at(dy=1))
    b_left = cp.start(by_s.at[1], by_r.at[1], me.at(dy=-1))

    z_right, z_left = z_step(2)

    x_right.wait_recv()
    x_left.wait_recv()

    def add_x2(i, carry):
        x_y[i] = (c_sum[0, i].astype(F32) + x_r[0, i].astype(F32) + x_r[1, i].astype(F32)).astype(BF16)
        return carry

    lax.fori_loop(0, NY, add_x2, 0)
    ct, cl = pl.ds(0, 256), pl.ds(256, 256)
    c_right = cp.start(x_y.at[far, ct], cy_2.at[ct], me.at(dy=1))
    c_left = cp.start(x_y.at[far, cl], cy_2.at[cl], me.at(dy=-1))

    z_right, z_left = z_step(1)

    c_right.wait_recv()
    c_left.wait_recv()
    cy_s[0, ct] = (x_y[up, ct].astype(F32) + cy_2[ct].astype(F32)).astype(BF16)
    cy_s[0, cl] = x_y[up, cl]
    cy_s[1, cl] = (x_y[down, cl].astype(F32) + cy_2[cl].astype(F32)).astype(BF16)
    cy_s[1, ct] = x_y[down, ct]
    c_right = cp.start(cy_s.at[0], cy_r.at[0], me.at(dy=1))
    c_left = cp.start(cy_s.at[1], cy_r.at[1], me.at(dy=-1))

    combine(z)
    b_right.wait_recv()
    b_left.wait_recv()

    def add_b2(i, carry):
        rows = pl.ds(pl.multiple_of(i * 512, 512), 512)
        out_b[rows] = b_sum[y, rows].astype(F32) + by_r[0, rows].astype(F32) + by_r[1, rows].astype(F32)
        return carry

    lax.fori_loop(0, 4, add_b2, 0)
    z_right.wait_recv()
    z_left.wait_recv()
    out_h[...] = (hid[z] + zr_r[0].astype(F32) + zr_l[0].astype(F32)).astype(BF16)
    c_right.wait_recv()
    c_left.wait_recv()
    out_c[...] = x_y[y].astype(F32) + cy_r[0].astype(F32) + cy_r[1].astype(F32)
    cp.finish()


def reduce(back, place, hidden, gc, gb):
    vmem = pl.BlockSpec(memory_space=pltpu.VMEM)
    copies = 32
    bf = lambda *shape: pltpu.VMEM(shape, BF16)
    return pl.pallas_call(
        reduce_kernel,
        out_shape=(
            jax.ShapeDtypeStruct((DOC, D), BF16),
            jax.ShapeDtypeStruct((CL, 128), F32),
            jax.ShapeDtypeStruct((2048, 128), F32),
        ),
        in_specs=[vmem] * 5,
        out_specs=(vmem,) * 3,
        scratch_shapes=[
            bf(NZ, 128, D), pltpu.VMEM((NZ, DOC, D), F32),
            bf(4, DOC, D), bf(4, DOC, D), bf(4, DOC, D), bf(4, DOC, D),
            bf(NY, NX, CL, 128), bf(NX, NY, CL, 128), bf(2, CL, 128), bf(2, CL, 128),
            bf(2, NY, CL, 128), bf(2, NY, CL, 128), bf(NY, CL, 128), bf(CL, 128), bf(2, CL, 128), bf(2, CL, 128),
            bf(NY, 2048, 128), bf(NY, 2048, 128), bf(2048, 128), bf(2, 2048, 128), bf(2, 2048, 128),
            pltpu.SemaphoreType.DMA((copies,)),
            pltpu.SemaphoreType.DMA((copies,)),
        ],
        compiler_params=pltpu.CompilerParams(
            collective_id=1, has_side_effects=True, vmem_limit_bytes=VMEM_LIMIT
        ),
    )(back, place, hidden, gc, gb)


def per_device(encoded, positive_clusters, cluster_weight, shortlist, positive_offsets, block_weight):
    scale = 1.0 / math.sqrt(DOC * NY * NC * NX * NZ)
    label = lax.axis_index("label")
    x, z = label // NZ, label % NZ
    meta = jnp.concatenate(
        [positive_clusters.T, shortlist.T, positive_offsets.T, jnp.zeros((4, DOC), jnp.int32)], axis=0
    )
    docs, wrel, metas, arr, tgt, place = gather(encoded, cluster_weight, meta)
    rows = docs.reshape(NZ * DOC, D)
    weight = wrel.reshape(NX * CL, D)
    scores = dot(rows, weight, ((1,), (1,)))
    group = (x + jnp.arange(NX, dtype=jnp.int32)) % NX * NZ + z
    ids = (group[:, None] * CL + jnp.arange(CL, dtype=jnp.int32)[None, :]).reshape(-1)
    positives = metas[:, 0:4, :].transpose(0, 2, 1).reshape(NZ * DOC, 4)
    hits = jnp.any(positives[:, :, None] == ids[None, None, :], axis=1)
    delta = (jax.nn.sigmoid(scores) - hits.astype(F32)).astype(BF16)
    grad_c = (dot(delta, rows, ((0,), (0,))) * scale).astype(BF16)
    hidden = dot(delta, weight, ((1,), (0,))).reshape(NZ, DOC, D)

    own = jnp.stack([tgt[e][:, ((NX - e) % NX) * 32:((NX - e) % NX) * 32 + 32] for e in range(NX)])
    own = own.reshape(NX, NZ, 2, 16).transpose(3, 0, 1, 2).reshape(16, 64).astype(jnp.int32)
    arrived = arr.reshape(NX, NZ, 2, 16, D).transpose(3, 0, 1, 2, 4).reshape(16, 64, D)
    scores = jnp.einsum("bsd,bld->bsl", arrived, block_weight, preferred_element_type=F32)
    target = (own[..., None] - 1 == jnp.arange(LBL, dtype=jnp.int32)).astype(F32)
    delta = jnp.where((own > 0)[..., None], jax.nn.sigmoid(scores) - target, 0.0).astype(BF16)
    back = jnp.einsum("bsl,bld->bsd", delta, block_weight, preferred_element_type=F32).astype(BF16)
    grad_b = jnp.einsum("bsl,bsd->bld", delta, arrived, preferred_element_type=F32)
    back = back.reshape(16, NX, NZ, 2, D).transpose(1, 2, 3, 0, 4).reshape(NX, NZ, 32, D)
    grad_b = (grad_b * scale).astype(BF16).reshape(2048, NY, NC, 128).transpose(1, 2, 0, 3)
    grad_c = grad_c.reshape(NX, CL, NY, NC, 128).transpose(2, 3, 0, 1, 4)
    out_h, out_c, out_b = reduce(back, place, hidden, grad_c, grad_b)
    return out_h, out_c, out_b.reshape(16, LBL, 128)


def solution(mesh):
    placed = (
        P(("dp", "label"), None),
        P(("dp", "label"), None),
        P("label", None),
        P(("dp", "label"), None),
        P(("dp", "label"), None),
        P("label", None, None),
    )
    return jax.shard_map(
        per_device,
        mesh=mesh,
        in_specs=placed,
        out_specs=(P(("dp", "label"), None), P("label", "dp"), P("label", None, "dp")),
        check_vma=False,
    )
```

```python
import math

import jax
import jax.numpy as jnp
from jax import lax
from jax.experimental import pallas as pl
from jax.experimental.pallas import tpu as pltpu
from jax.sharding import PartitionSpec as P

MESH = pl.DeviceIdType.MESH
F32, BF16 = jnp.float32, jnp.bfloat16
NY, NC, NX, NZ = 4, 2, 4, 8
DOC, D, CL, LBL = 128, 1024, 512, 128
VMEM_LIMIT = 60 * 1024 * 1024


class Spot:
    def __init__(self):
        dp, label = lax.axis_index("dp"), lax.axis_index("label")
        self.y, self.c = dp // NC, dp % NC
        self.x, self.z = label // NZ, label % NZ

    def at(self, dx=0, dy=0, dz=0, dc=0):
        y, x, z = (self.y + dy) % NY, (self.x + dx) % NX, (self.z + dz) % NZ
        return (y * NC + (self.c + dc) % NC, x * NZ + z)


def greet(others):
    barrier = pltpu.get_barrier_semaphore()
    for other in others:
        pl.semaphore_signal(barrier, inc=1, device_id=other, device_id_type=MESH)
    pl.semaphore_wait(barrier, len(others))


class Copies:
    def __init__(self, send, recv):
        self.send, self.recv, self.used, self.sent = send, recv, 0, []

    def start(self, src, dst, device):
        i = self.used
        self.used += 1
        copy = pltpu.make_async_remote_copy(
            src_ref=src, dst_ref=dst, send_sem=self.send.at[i], recv_sem=self.recv.at[i],
            device_id=device, device_id_type=MESH,
        )
        copy.start()
        self.sent.append(copy)
        return copy

    def finish(self):
        for copy in self.sent:
            copy.wait_send()


def dot(a, b, dims):
    return lax.dot_general(a, b, (dims, ((), ())), preferred_element_type=F32)


def sigmoid(v):
    return 1.0 / (1.0 + jnp.exp(-v))


def iota(shape, dim):
    return lax.broadcasted_iota(jnp.int32, shape, dim)


def kernel(
    enc, w, meta, bw_hbm, out_h, out_c, out_b,
    docs, docs_t, wrel, bw, metas, pos_t, arr, tgt, off, place, disp, rows_p, delta,
    ret, hid, zs_r, zs_l, zr_r, zr_l,
    gc, c_in, x_r2, x_l2, x_s, x_r, x_y, cy_2, cy_s, cy_r,
    gb, b_in, by_2, by_s, by_r, send, recv, local,
):
    me = Spot()
    x, y, z, c = me.x, me.y, me.z, me.c
    scale = 1.0 / math.sqrt(DOC * NY * NC * NX * NZ)
    own = [
        pltpu.make_async_copy(enc, docs.at[z], local.at[0]),
        pltpu.make_async_copy(meta, metas.at[z], local.at[1]),
        pltpu.make_async_copy(w, wrel.at[0], local.at[2]),
        pltpu.make_async_copy(bw_hbm, bw, local.at[3]),
    ]
    for copy in own:
        copy.start()
    greet(
        [me.at(dz=i) for i in range(1, NZ)] + [me.at(dx=i) for i in range(1, NX)]
        + [me.at(dy=1), me.at(dy=-1), me.at(dc=1)]
    )
    cp = Copies(send, recv)
    half = DOC // 2
    right = cp.start(enc, docs.at[z], me.at(dz=1))
    left = cp.start(enc, docs.at[z], me.at(dz=-1))
    got_meta = [None] + [cp.start(meta, metas.at[z], me.at(dz=i)) for i in range(1, NZ)]
    w_right = cp.start(w.at[y, c], wrel.at[3, y, c], me.at(dx=1))
    w_left = cp.start(w.at[y, c], wrel.at[1, y, c], me.at(dx=-1))

    slot = iota((128, 128), 0)
    lane = iota((128, 128), 1)
    block = (((x + (slot >> 5)) & 3) * NZ + z) * 16 + (slot & 15)
    turn = ((slot >> 4) & 1).astype(F32)
    upper = jnp.where(slot < lane, 1.0, 0.0).astype(BF16)
    eye = jnp.where(slot == lane, 1.0, 0.0).astype(BF16)
    row8 = iota((8, 128), 0)
    tgt[0] = jnp.zeros((8, 128), F32)
    arrivals = [[] for _ in range(NX)]

    def dispatch(zs):
        info = metas[zs]
        named = jnp.zeros((128, 128), F32)
        offset = jnp.zeros((128, 128), F32)
        for k in range(4):
            hit = info[4 + k:5 + k, :] == block
            named = jnp.where(hit, 1.0, named)
            offset = jnp.where(hit, (info[8 + k:9 + k, :] + 1).astype(F32), offset)
        rank = dot(named.astype(BF16), upper, ((1,), (0,)))
        chosen = jnp.where(rank == turn, named, 0.0)
        place[zs] = chosen.astype(BF16)
        disp[zs] = dot(chosen.astype(BF16), docs[zs], ((1,), (0,))).astype(BF16)
        for d in range(1, NX):
            arrivals[NX - d].append(
                cp.start(disp.at[zs, pl.ds(d * 32, 32)], arr.at[NX - d, zs], me.at(dx=d))
            )
        arr[0, zs] = disp[zs, 0:32]
        pick = jnp.where(row8 == zs, 1.0, 0.0).astype(BF16)
        tgt[0] += dot(pick, (chosen * offset).astype(BF16), ((1,), (1,)))

    def prepare(zs):
        columns = pl.ds(pl.multiple_of(zs * 128, 128), 128)
        for j in range(D // 128):
            docs_t[pl.ds(j * 128, 128), columns] = dot(
                eye, docs[zs, :, j * 128:(j + 1) * 128], ((1,), (1,))
            ).astype(BF16)
        pos_t[columns, :] = jnp.transpose(metas[zs].astype(F32), (1, 0))

    def first(tile, pos, base):
        ids = (base + iota((1, tile.shape[1]), 1)).astype(F32)
        hit = pos[:, 0:1] == ids
        for k in range(1, 4):
            hit = hit | (pos[:, k:k + 1] == ids)
        return (sigmoid(tile) - jnp.where(hit, 1.0, 0.0)).astype(BF16)

    def own_group(zs):
        rows = pl.ds(pl.multiple_of(zs * 128, 128), 128)
        tile = dot(docs[zs], wrel[0].reshape(CL, D), ((1,), (1,)))
        delta[rows, 0:CL] = first(tile, pos_t[rows, :], (x * NZ + z) * CL)

    own[0].wait()
    own[1].wait()
    dispatch(z)
    prepare(z)
    own[2].wait()
    own_group(z)
    groups = pl.ds(1, 3)
    for h in range(1, NZ // 2):
        from_left, from_right = (z - h) % NZ, (z + h) % NZ
        right.wait_recv()
        left.wait_recv()
        if h + 1 < NZ // 2:
            right = cp.start(docs.at[from_left], docs.at[from_left], me.at(dz=1))
            left = cp.start(docs.at[from_right], docs.at[from_right], me.at(dz=-1))
        else:
            right = cp.start(
                docs.at[from_left, pl.ds(0, half)], docs.at[from_left, pl.ds(0, half)], me.at(dz=1)
            )
            left = cp.start(
                docs.at[from_right, pl.ds(half, half)], docs.at[from_right, pl.ds(half, half)], me.at(dz=-1)
            )
        if h == 1:
            w_right.wait_recv()
            w_left.wait_recv()
            w_right = cp.start(w_part(wrel, 3, y, c, 0), w_part(wrel, 2, y, c, 0), me.at(dx=1))
            w_left = cp.start(w_part(wrel, 1, y, c, 1), w_part(wrel, 2, y, c, 1), me.at(dx=-1))
        if h == 2:
            w_right.wait_recv()
            w_left.wait_recv()
            y_right = cp.start(wrel.at[groups, y, c], wrel.at[groups, y, c], me.at(dy=1))
            y_left = cp.start(wrel.at[groups, y, c], wrel.at[groups, y, c], me.at(dy=-1))
            sib = [cp.start(wrel.at[groups, y, c], wrel.at[groups, y, c], me.at(dc=1))]
        if h == 3:
            y_right.wait_recv()
            y_left.wait_recv()
            yl, yr = (y - 1) % NY, (y + 1) % NY
            sib.append(cp.start(wrel.at[groups, yl, c], wrel.at[groups, yl, c], me.at(dc=1)))
            sib.append(cp.start(wrel.at[groups, yr, c], wrel.at[groups, yr, c], me.at(dc=1)))
            a, b = pl.ds(0, 32), pl.ds(32, 32)
            y_right = cp.start(wrel.at[groups, yl, c, a], wrel.at[groups, yl, c, a], me.at(dy=1))
            y_left = cp.start(wrel.at[groups, yr, c, b], wrel.at[groups, yr, c, b], me.at(dy=-1))
        got_meta[h].wait_recv()
        dispatch(from_left)
        got_meta[NZ - h].wait_recv()
        dispatch(from_right)
        for zs in (from_left, from_right):
            prepare(zs)
            own_group(zs)
    y_right.wait_recv()
    y_left.wait_recv()
    far = (y + 2) % NY
    sib.append(cp.start(wrel.at[groups, far, c], wrel.at[groups, far, c], me.at(dc=1)))
    right.wait_recv()
    left.wait_recv()
    got_meta[NZ // 2].wait_recv()
    opposite = (z + NZ // 2) % NZ
    dispatch(opposite)
    for d in range(1, NX):
        arrivals[NX - d].append(cp.start(tgt.at[0], tgt.at[NX - d], me.at(dx=d)))
    prepare(opposite)
    own_group(opposite)

    to, fro = iota((256, 256), 0), iota((256, 256), 1)
    moved = ((to >> 1) & 7) * 32 + (to & 1) * 16 + (to >> 4)
    shuffle = jnp.where(fro == moved, 1.0, 0.0).astype(BF16)
    offs = jnp.zeros((16, 64), F32)
    for e in range(NX):
        for copy in arrivals[e]:
            copy.wait_recv()
        rows = dot(shuffle, arr[e].reshape(256, D), ((1,), (0,))).astype(BF16)
        rows_p[:, e * 16:(e + 1) * 16, :] = rows.reshape(16, 16, D)
        for t in range(2):
            at = ((NX - e) % NX) * 32 + t * 16
            take = jnp.where(iota((16, 128), 1) == iota((16, 128), 0) + at, 1.0, 0.0).astype(BF16)
            put = jnp.where(iota((8, 64), 1) == iota((8, 64), 0) * 2 + (e * 16 + t), 1.0, 0.0).astype(BF16)
            taken = dot(take, tgt[e].astype(BF16), ((1,), (1,))).astype(BF16)
            offs = offs + dot(taken, put, ((1,), (0,)))
    off[...] = offs
    own[3].wait()

    def second(b, carry):
        rows, weight = rows_p[b], bw[b]
        scores = dot(weight, rows, ((1,), (1,)))
        wanted = off[pl.ds(b, 1), :]
        target = jnp.where(iota((LBL, 64), 0).astype(F32) + 1.0 == wanted, 1.0, 0.0)
        dt = jnp.where(wanted > 0.0, sigmoid(scores) - target, 0.0).astype(BF16)
        grad = dot(dt, rows, ((1,), (0,))) * scale
        at = pl.ds(pl.multiple_of(b * LBL, LBL), LBL)
        for j in range(NY * NC):
            gb[j // NC, j % NC, at, :] = grad[:, j * 128:(j + 1) * 128].astype(BF16)
        rows_p[b] = dot(dt, weight, ((0,), (0,))).astype(BF16)
        return carry

    lax.fori_loop(0, 16, second, 0)
    returns = []
    for e in (2, 1, 3, 0):
        rows = dot(shuffle, rows_p[:, e * 16:(e + 1) * 16, :].reshape(256, D), ((0,), (0,)))
        arr[e] = rows.astype(BF16).reshape(NZ, 32, D)
        if e > 0:
            dst = ret.at[pl.ds(0, NZ), pl.ds((NX - e) * 32, 32)]
            returns.append(cp.start(arr.at[e], dst, me.at(dx=e)))
        else:
            for i in range(NZ):
                ret[i, 0:32] = arr[0, i]
    b_core = cp.start(gb.at[pl.ds(0, NY), 1 - c], b_in, me.at(dc=1))

    for copy in sib:
        copy.wait_recv()

    def scores_one(t, carry):
        g, h = t // 2, t % 2
        weight = wrel[g, pl.ds(h * 2, 2)].reshape(256, D)
        tile = dot(docs[...].reshape(NZ * DOC, D), weight, ((1,), (1,)))
        base = (((x + g) % NX) * NZ + z) * CL + h * 256
        delta[:, pl.ds(pl.multiple_of(t * 256, 256), 256)] = first(tile, pos_t[...], base)
        return carry

    lax.fori_loop(2, 8, scores_one, 0)

    b_core.wait_recv()

    def add_block(i, carry):
        rows = pl.ds(pl.multiple_of((i % 4) * 512, 512), 512)
        gb[i // 4, c, rows] = (gb[i // 4, c, rows].astype(F32) + b_in[i // 4, rows].astype(F32)).astype(BF16)
        return carry

    lax.fori_loop(0, 16, add_block, 0)
    top, low = pl.ds(0, 1024), pl.ds(1024, 1024)
    b_right = cp.start(gb.at[far, c, top], by_2.at[top], me.at(dy=1))
    b_left = cp.start(gb.at[far, c, low], by_2.at[low], me.at(dy=-1))

    def grad_one(t, carry):
        columns = pl.ds(pl.multiple_of(t * 256, 256), 256)
        grad = dot(docs_t[...], delta[:, columns], ((1,), (0,))) * scale
        at = pl.ds(pl.multiple_of((t % 2) * 256, 256), 256)
        gc[:, :, t // 2, :, at] = grad.astype(BF16).reshape(NY, NC, 128, 256)
        return carry

    lax.fori_loop(0, 8, grad_one, 0)
    c_core = cp.start(gc.at[pl.ds(0, NY), 1 - c], c_in, me.at(dc=1))

    up, down = (y + 1) % NY, (y - 1) % NY
    b_right.wait_recv()
    b_left.wait_recv()

    def add_b(i, carry):
        rows = pl.ds(pl.multiple_of(i * 512, 512), 512)
        other = pl.ds(pl.multiple_of(i * 512 + 1024, 512), 512)
        by_s[0, rows] = (gb[up, c, rows].astype(F32) + by_2[rows].astype(F32)).astype(BF16)
        by_s[0, other] = gb[up, c, other]
        by_s[1, other] = (gb[down, c, other].astype(F32) + by_2[other].astype(F32)).astype(BF16)
        by_s[1, rows] = gb[down, c, rows]
        return carry

    lax.fori_loop(0, 2, add_b, 0)
    b_right = cp.start(by_s.at[0], by_r.at[0], me.at(dy=1))
    b_left = cp.start(by_s.at[1], by_r.at[1], me.at(dy=-1))

    def hidden_one(t, carry):
        columns = pl.ds(pl.multiple_of(t * 256, 256), 256)
        weight = wrel[:, :, :, :, columns].reshape(NX * CL, 256)
        hid[:, :, columns] = dot(delta[...], weight, ((1,), (0,))).reshape(NZ, DOC, 256)
        return carry

    lax.fori_loop(0, 4, hidden_one, 0)

    c_core.wait_recv()

    def add_cluster(i, carry):
        t, g = i // 4, i % 4
        gc[t, c, g] = (gc[t, c, g].astype(F32) + c_in[t, g].astype(F32)).astype(BF16)
        return carry

    lax.fori_loop(0, 16, add_cluster, 0)
    x_right = cp.start(gc.at[pl.ds(0, 2), c, 2], x_r2, me.at(dx=1))
    x_left = cp.start(gc.at[pl.ds(2, 2), c, 2], x_l2, me.at(dx=-1))

    for copy in returns:
        copy.wait_recv()

    def combine(t):
        hid[t] = hid[t] + dot(place[t], ret[t], ((0,), (0,)))

    combine(opposite)
    zs_r[3, 0:half] = hid[opposite, 0:half].astype(BF16)
    zs_l[3, half:DOC] = hid[opposite, half:DOC].astype(BF16)
    a, b = pl.ds(0, half), pl.ds(half, half)
    z_right = cp.start(zs_r.at[3, a], zr_r.at[3, a], me.at(dz=1))
    z_left = cp.start(zs_l.at[3, b], zr_l.at[3, b], me.at(dz=-1))

    def z_step(h):
        right, left = (z + h) % NZ, (z - h) % NZ
        combine(right)
        combine(left)
        z_right.wait_recv()
        z_left.wait_recv()
        if h == 3:
            zs_r[2, 0:half] = (hid[right, 0:half] + zr_r[3, 0:half].astype(F32)).astype(BF16)
            zs_r[2, half:DOC] = hid[right, half:DOC].astype(BF16)
            zs_l[2, half:DOC] = (hid[left, half:DOC] + zr_l[3, half:DOC].astype(F32)).astype(BF16)
            zs_l[2, 0:half] = hid[left, 0:half].astype(BF16)
        else:
            zs_r[h - 1] = (hid[right] + zr_r[h].astype(F32)).astype(BF16)
            zs_l[h - 1] = (hid[left] + zr_l[h].astype(F32)).astype(BF16)
        return (
            cp.start(zs_r.at[h - 1], zr_r.at[h - 1], me.at(dz=1)),
            cp.start(zs_l.at[h - 1], zr_l.at[h - 1], me.at(dz=-1)),
        )

    z_right, z_left = z_step(3)

    x_right.wait_recv()
    x_left.wait_recv()

    def add_x(i, carry):
        x_s[0, i] = (gc[i, c, 1].astype(F32) + x_r2[i].astype(F32)).astype(BF16)
        x_s[0, i + 2] = gc[i + 2, c, 1]
        x_s[1, i + 2] = (gc[i + 2, c, 3].astype(F32) + x_l2[i].astype(F32)).astype(BF16)
        x_s[1, i] = gc[i, c, 3]
        return carry

    lax.fori_loop(0, 2, add_x, 0)
    x_right = cp.start(x_s.at[0], x_r.at[0], me.at(dx=1))
    x_left = cp.start(x_s.at[1], x_r.at[1], me.at(dx=-1))

    z_right, z_left = z_step(2)

    x_right.wait_recv()
    x_left.wait_recv()

    def add_x2(i, carry):
        x_y[i] = (gc[i, c, 0].astype(F32) + x_r[0, i].astype(F32) + x_r[1, i].astype(F32)).astype(BF16)
        return carry

    lax.fori_loop(0, NY, add_x2, 0)
    ct, cl = pl.ds(0, 64), pl.ds(64, 64)
    c_right = cp.start(x_y.at[far, ct], cy_2.at[ct], me.at(dy=1))
    c_left = cp.start(x_y.at[far, cl], cy_2.at[cl], me.at(dy=-1))

    z_right, z_left = z_step(1)

    c_right.wait_recv()
    c_left.wait_recv()
    cy_s[0, ct] = (x_y[up, ct].astype(F32) + cy_2[ct].astype(F32)).astype(BF16)
    cy_s[0, cl] = x_y[up, cl]
    cy_s[1, cl] = (x_y[down, cl].astype(F32) + cy_2[cl].astype(F32)).astype(BF16)
    cy_s[1, ct] = x_y[down, ct]
    c_right = cp.start(cy_s.at[0], cy_r.at[0], me.at(dy=1))
    c_left = cp.start(cy_s.at[1], cy_r.at[1], me.at(dy=-1))

    combine(z)
    b_right.wait_recv()
    b_left.wait_recv()

    def add_b2(i, carry):
        rows = pl.ds(pl.multiple_of(i * 512, 512), 512)
        out_b[rows] = gb[y, c, rows].astype(F32) + by_r[0, rows].astype(F32) + by_r[1, rows].astype(F32)
        return carry

    lax.fori_loop(0, 4, add_b2, 0)
    z_right.wait_recv()
    z_left.wait_recv()
    out_h[...] = (hid[z] + zr_r[0].astype(F32) + zr_l[0].astype(F32)).astype(BF16)
    c_right.wait_recv()
    c_left.wait_recv()
    out_c[...] = x_y[y].astype(F32) + cy_r[0].astype(F32) + cy_r[1].astype(F32)
    cp.finish()


def w_part(wrel, group, y, c, part):
    return wrel.at[group, y, c, pl.ds(part * 32, 32)]


def per_device(encoded, positive_clusters, cluster_weight, shortlist, positive_offsets, block_weight):
    meta = jnp.concatenate(
        [positive_clusters.T, shortlist.T, positive_offsets.T, jnp.zeros((4, DOC), jnp.int32)], axis=0
    )
    vmem = pl.BlockSpec(memory_space=pltpu.VMEM)
    hbm = pl.BlockSpec(memory_space=pl.ANY)
    bf = lambda *shape: pltpu.VMEM(shape, BF16)
    f32 = lambda *shape: pltpu.VMEM(shape, F32)
    copies = 88
    out_h, out_c, out_b = pl.pallas_call(
        kernel,
        out_shape=(
            jax.ShapeDtypeStruct((DOC, D), BF16),
            jax.ShapeDtypeStruct((128, CL), F32),
            jax.ShapeDtypeStruct((2048, 128), F32),
        ),
        in_specs=[hbm] * 4,
        out_specs=(vmem,) * 3,
        scratch_shapes=[
            bf(NZ, DOC, D), bf(D, NZ * DOC), bf(NX, NY, NC, 64, D), bf(16, LBL, D),
            pltpu.VMEM((NZ, 16, 128), jnp.int32), f32(NZ * DOC, 16), bf(NX, NZ, 32, D), f32(NX, NZ, 128),
            f32(16, 64), bf(NZ, 128, 128), bf(NZ, 128, D), bf(16, 64, D), bf(NZ * DOC, NX * CL),
            bf(NZ, 128, D), f32(NZ, DOC, D), bf(4, DOC, D), bf(4, DOC, D), bf(4, DOC, D), bf(4, DOC, D),
            bf(NY, NC, NX, 128, CL), bf(NY, NX, 128, CL), bf(2, 128, CL), bf(2, 128, CL),
            bf(2, NY, 128, CL), bf(2, NY, 128, CL), bf(NY, 128, CL), bf(128, CL), bf(2, 128, CL), bf(2, 128, CL),
            bf(NY, NC, 2048, 128), bf(NY, 2048, 128), bf(2048, 128), bf(2, 2048, 128), bf(2, 2048, 128),
            pltpu.SemaphoreType.DMA((copies,)),
            pltpu.SemaphoreType.DMA((copies,)),
            pltpu.SemaphoreType.DMA((4,)),
        ],
        compiler_params=pltpu.CompilerParams(
            collective_id=0, has_side_effects=True, vmem_limit_bytes=VMEM_LIMIT
        ),
    )(encoded, cluster_weight.reshape(NY, NC, 64, D), meta, block_weight)
    return out_h, out_c.T, out_b.reshape(16, LBL, 128)


def solution(mesh):
    placed = (
        P(("dp", "label"), None),
        P(("dp", "label"), None),
        P("label", None),
        P(("dp", "label"), None),
        P(("dp", "label"), None),
        P("label", None, None),
    )
    return jax.shard_map(
        per_device,
        mesh=mesh,
        in_specs=placed,
        out_specs=(P(("dp", "label"), None), P("label", "dp"), P("label", None, "dp")),
        check_vma=False,
    )
```

```python
import math

import jax
import jax.numpy as jnp
from jax import lax
from jax.experimental import pallas as pl
from jax.experimental.pallas import tpu as pltpu
from jax.sharding import PartitionSpec as P

MESH = pl.DeviceIdType.MESH
F32, BF16 = jnp.float32, jnp.bfloat16
NY, NC, NX, NZ = 4, 2, 4, 8
DOC, D, CL, LBL = 128, 1024, 512, 128
VMEM_LIMIT = 60 * 1024 * 1024


class Spot:
    def __init__(self):
        dp, label = lax.axis_index("dp"), lax.axis_index("label")
        self.y, self.c = dp // NC, dp % NC
        self.x, self.z = label // NZ, label % NZ

    def at(self, dx=0, dy=0, dz=0, dc=0):
        y, x, z = (self.y + dy) % NY, (self.x + dx) % NX, (self.z + dz) % NZ
        return (y * NC + (self.c + dc) % NC, x * NZ + z)


class Copies:
    def __init__(self, send, recv):
        self.send, self.recv, self.used, self.sent = send, recv, 0, []

    def start(self, src, dst, device):
        i = self.used
        self.used += 1
        copy = pltpu.make_async_remote_copy(
            src_ref=src, dst_ref=dst, send_sem=self.send.at[i], recv_sem=self.recv.at[i],
            device_id=device, device_id_type=MESH,
        )
        copy.start()
        self.sent.append(copy)
        return copy

    def finish(self):
        for copy in self.sent:
            copy.wait_send()


def dot(a, b, dims):
    return lax.dot_general(a, b, (dims, ((), ())), preferred_element_type=F32)


def sigmoid(v):
    return 1.0 / (1.0 + jnp.exp(-v))


def iota(shape, dim):
    return lax.broadcasted_iota(jnp.int32, shape, dim)


def kernel(
    enc, w, pos, listed, offsets, bw_hbm, out_h, out_c, out_b,
    docs, docs_t, wrel, bw, metas, pos_t, arr, tgt, off, place, disp, rows_p, delta,
    ret, hid, zs_r, zs_l, zr_r, zr_l,
    gc, c_in, cy_2, cy_s, cy_r, c_y, x_2, x_s, x_r,
    gb, b_in, by_2, by_s, by_r, o_h, o_c, o_b, send, recv, local,
):
    me = Spot()
    x, y, z, c = me.x, me.y, me.z, me.c
    scale = 1.0 / math.sqrt(DOC * NY * NC * NX * NZ)
    own = [
        pltpu.make_async_copy(enc, docs.at[z], local.at[0]),
        pltpu.make_async_copy(pos, metas.at[z, pl.ds(0, 4)], local.at[1]),
        pltpu.make_async_copy(listed, metas.at[z, pl.ds(4, 4)], local.at[2]),
        pltpu.make_async_copy(offsets, metas.at[z, pl.ds(8, 4)], local.at[3]),
        pltpu.make_async_copy(w, wrel.at[0], local.at[4]),
        pltpu.make_async_copy(bw_hbm, bw, local.at[5]),
    ]
    for copy in own:
        copy.start()
    metas[z, 12:16] = jnp.zeros((4, 128), jnp.int32)
    others = (
        [me.at(dz=i) for i in range(1, NZ)] + [me.at(dx=i) for i in range(1, NX)]
        + [me.at(dy=1), me.at(dy=-1), me.at(dc=1)]
    )
    barrier = pltpu.get_barrier_semaphore()
    for other in others:
        pl.semaphore_signal(barrier, inc=1, device_id=other, device_id_type=MESH)
    cp = Copies(send, recv)
    half = DOC // 2

    slot = iota((128, 128), 0)
    lane = iota((128, 128), 1)
    block = (((x + (slot >> 5)) & 3) * NZ + z) * 16 + (slot & 15)
    turn = ((slot >> 4) & 1).astype(F32)
    upper = jnp.where(slot < lane, 1.0, 0.0).astype(BF16)
    eye = jnp.where(slot == lane, 1.0, 0.0).astype(BF16)
    row8 = iota((8, 128), 0)
    tgt[0] = jnp.zeros((8, 128), F32)
    arrivals = [[] for _ in range(NX)]

    def choose(zs):
        info = metas[zs]
        named = jnp.zeros((128, 128), F32)
        offset = jnp.zeros((128, 128), F32)
        for k in range(4):
            hit = info[4 + k:5 + k, :] == block
            named = jnp.where(hit, 1.0, named)
            offset = jnp.where(hit, (info[8 + k:9 + k, :] + 1).astype(F32), offset)
        rank = dot(named.astype(BF16), upper, ((1,), (0,)))
        chosen = jnp.where(rank == turn, named, 0.0)
        place[zs] = chosen.astype(BF16)
        disp[zs] = dot(chosen.astype(BF16), docs[zs], ((1,), (0,))).astype(BF16)
        pick = jnp.where(row8 == zs, 1.0, 0.0).astype(BF16)
        tgt[0] += dot(pick, (chosen * offset).astype(BF16), ((1,), (1,)))

    def hand_on(zs):
        for d in (2, 1, 3):
            arrivals[NX - d].append(
                cp.start(disp.at[zs, pl.ds(d * 32, 32)], arr.at[NX - d, zs], me.at(dx=d))
            )
        arr[0, zs] = disp[zs, 0:32]

    def dispatch(zs):
        choose(zs)
        hand_on(zs)

    def prepare(zs):
        columns = pl.ds(pl.multiple_of(zs * 128, 128), 128)
        for j in range(D // 128):
            docs_t[pl.ds(j * 128, 128), columns] = dot(
                eye, docs[zs, :, j * 128:(j + 1) * 128], ((1,), (1,))
            ).astype(BF16)
        pos_t[columns, :] = jnp.transpose(metas[zs].astype(F32), (1, 0))

    def first(tile, pos, base):
        ids = (base + iota((1, tile.shape[1]), 1)).astype(F32)
        hit = pos[:, 0:1] == ids
        for k in range(1, 4):
            hit = hit | (pos[:, k:k + 1] == ids)
        return (sigmoid(tile) - jnp.where(hit, 1.0, 0.0)).astype(BF16)

    def own_group(zs):
        rows = pl.ds(pl.multiple_of(zs * 128, 128), 128)
        tile = dot(docs[zs], wrel[0].reshape(CL, D), ((1,), (1,)))
        delta[rows, 0:CL] = first(tile, pos_t[rows, :], (x * NZ + z) * CL)

    for i in range(4):
        own[i].wait()
    choose(z)
    prepare(z)
    pl.semaphore_wait(barrier, len(others))
    right = cp.start(docs.at[z], docs.at[z], me.at(dz=1))
    left = cp.start(docs.at[z], docs.at[z], me.at(dz=-1))
    w_right = cp.start(w.at[y, c], wrel.at[3, y, c], me.at(dx=1))
    w_left = cp.start(w.at[y, c], wrel.at[1, y, c], me.at(dx=-1))
    got_meta = [None] + [cp.start(metas.at[z], metas.at[z], me.at(dz=i)) for i in range(1, NZ)]
    hand_on(z)
    own[4].wait()
    own_group(z)
    groups = pl.ds(1, 3)
    w_right.wait_recv()
    w_left.wait_recv()
    w_right = cp.start(w_part(wrel, 3, y, c, 0), w_part(wrel, 2, y, c, 0), me.at(dx=1))
    w_left = cp.start(w_part(wrel, 1, y, c, 1), w_part(wrel, 2, y, c, 1), me.at(dx=-1))
    for h in range(1, NZ // 2):
        from_left, from_right = (z - h) % NZ, (z + h) % NZ
        right.wait_recv()
        left.wait_recv()
        if h + 1 < NZ // 2:
            right = cp.start(docs.at[from_left], docs.at[from_left], me.at(dz=1))
            left = cp.start(docs.at[from_right], docs.at[from_right], me.at(dz=-1))
        else:
            right = cp.start(
                docs.at[from_left, pl.ds(0, half)], docs.at[from_left, pl.ds(0, half)], me.at(dz=1)
            )
            left = cp.start(
                docs.at[from_right, pl.ds(half, half)], docs.at[from_right, pl.ds(half, half)], me.at(dz=-1)
            )
        if h == 1:
            w_right.wait_recv()
            w_left.wait_recv()
            y_right = cp.start(wrel.at[groups, y, c], wrel.at[groups, y, c], me.at(dy=1))
            y_left = cp.start(wrel.at[groups, y, c], wrel.at[groups, y, c], me.at(dy=-1))
            sib = [cp.start(wrel.at[groups, y, c], wrel.at[groups, y, c], me.at(dc=1))]
        got_meta[h].wait_recv()
        dispatch(from_left)
        got_meta[NZ - h].wait_recv()
        dispatch(from_right)
        for zs in (from_left, from_right):
            prepare(zs)
            own_group(zs)
        if h == 2:
            y_right.wait_recv()
            y_left.wait_recv()
            yl, yr = (y - 1) % NY, (y + 1) % NY
            a, b = pl.ds(0, 32), pl.ds(32, 32)
            y_right = cp.start(wrel.at[groups, yl, c, a], wrel.at[groups, yl, c, a], me.at(dy=1))
            y_left = cp.start(wrel.at[groups, yr, c, b], wrel.at[groups, yr, c, b], me.at(dy=-1))
            sib.append(cp.start(wrel.at[groups, yl, c], wrel.at[groups, yl, c], me.at(dc=1)))
            sib.append(cp.start(wrel.at[groups, yr, c], wrel.at[groups, yr, c], me.at(dc=1)))
        if h == 3:
            y_right.wait_recv()
            y_left.wait_recv()
            far = (y + 2) % NY
            sib.append(cp.start(wrel.at[groups, far, c], wrel.at[groups, far, c], me.at(dc=1)))
    right.wait_recv()
    left.wait_recv()
    got_meta[NZ // 2].wait_recv()
    opposite = (z + NZ // 2) % NZ
    dispatch(opposite)
    for d in range(1, NX):
        arrivals[NX - d].append(cp.start(tgt.at[0], tgt.at[NX - d], me.at(dx=d)))
    prepare(opposite)
    own_group(opposite)

    for copy in sib:
        copy.wait_recv()

    def scores_one(t, carry):
        g, h = t // 2, t % 2
        weight = wrel[g, pl.ds(h * 2, 2)].reshape(256, D)
        tile = dot(docs[...].reshape(NZ * DOC, D), weight, ((1,), (1,)))
        base = (((x + g) % NX) * NZ + z) * CL + h * 256
        delta[:, pl.ds(pl.multiple_of(t * 256, 256), 256)] = first(tile, pos_t[...], base)
        return carry

    lax.fori_loop(2, 8, scores_one, 0)

    def grad_one(t, carry):
        columns = pl.ds(pl.multiple_of(t * 256, 256), 256)
        grad = dot(docs_t[...], delta[:, columns], ((1,), (0,))) * scale
        at = pl.ds(pl.multiple_of((t % 2) * 256, 256), 256)
        gc[:, :, t // 2, :, at] = grad.astype(BF16).reshape(NY, NC, 128, 256)
        return carry

    c_core = []
    for g in range(NX):
        lax.fori_loop(2 * g, 2 * g + 2, grad_one, 0)
        c_core.append(
            cp.start(gc.at[pl.ds(0, NY), 1 - c, g], c_in.at[pl.ds(0, NY), g], me.at(dc=1))
        )


    to, fro = iota((256, 256), 0), iota((256, 256), 1)
    moved = ((to >> 1) & 7) * 32 + (to & 1) * 16 + (to >> 4)
    shuffle = jnp.where(fro == moved, 1.0, 0.0).astype(BF16)
    offs = jnp.zeros((16, 64), F32)
    for e in range(NX):
        for copy in arrivals[e]:
            copy.wait_recv()
        rows = dot(shuffle, arr[e].reshape(256, D), ((1,), (0,))).astype(BF16)
        rows_p[:, e * 16:(e + 1) * 16, :] = rows.reshape(16, 16, D)
        for t in range(2):
            at = ((NX - e) % NX) * 32 + t * 16
            take = jnp.where(iota((16, 128), 1) == iota((16, 128), 0) + at, 1.0, 0.0).astype(BF16)
            put = jnp.where(iota((8, 64), 1) == iota((8, 64), 0) * 2 + (e * 16 + t), 1.0, 0.0).astype(BF16)
            taken = dot(take, tgt[e].astype(BF16), ((1,), (1,))).astype(BF16)
            offs = offs + dot(taken, put, ((1,), (0,)))
    off[...] = offs
    own[5].wait()

    def second(b, carry):
        rows, weight = rows_p[b], bw[b]
        scores = dot(weight, rows, ((1,), (1,)))
        wanted = off[pl.ds(b, 1), :]
        target = jnp.where(iota((LBL, 64), 0).astype(F32) + 1.0 == wanted, 1.0, 0.0)
        dt = jnp.where(wanted > 0.0, sigmoid(scores) - target, 0.0).astype(BF16)
        grad = dot(dt, rows, ((1,), (0,))) * scale
        at = pl.ds(pl.multiple_of(b * LBL, LBL), LBL)
        for j in range(NY * NC):
            gb[j // NC, j % NC, at, :] = grad[:, j * 128:(j + 1) * 128].astype(BF16)
        rows_p[b] = dot(dt, weight, ((0,), (0,))).astype(BF16)
        return carry

    lax.fori_loop(0, 4, second, 0)

    up, down = (y + 1) % NY, (y - 1) % NY
    for copy in c_core:
        copy.wait_recv()

    def add_cluster(i, carry):
        t, g = i // 4, i % 4
        gc[t, c, g] = (gc[t, c, g].astype(F32) + c_in[t, g].astype(F32)).astype(BF16)
        return carry

    lax.fori_loop(0, 16, add_cluster, 0)
    first_two, last_two = pl.ds(0, 2), pl.ds(2, 2)
    c_right = cp.start(gc.at[far, c, first_two], cy_2.at[first_two], me.at(dy=1))
    c_left = cp.start(gc.at[far, c, last_two], cy_2.at[last_two], me.at(dy=-1))

    lax.fori_loop(4, 13, second, 0)
    c_right.wait_recv()
    c_left.wait_recv()

    def add_c(i, carry):
        cy_s[0, i] = (gc[up, c, i].astype(F32) + cy_2[i].astype(F32)).astype(BF16)
        cy_s[0, i + 2] = gc[up, c, i + 2]
        cy_s[1, i + 2] = (gc[down, c, i + 2].astype(F32) + cy_2[i + 2].astype(F32)).astype(BF16)
        cy_s[1, i] = gc[down, c, i]
        return carry

    lax.fori_loop(0, 2, add_c, 0)
    c_right = cp.start(cy_s.at[0], cy_r.at[0], me.at(dy=1))
    c_left = cp.start(cy_s.at[1], cy_r.at[1], me.at(dy=-1))

    lax.fori_loop(13, 16, second, 0)
    b_core = cp.start(gb.at[pl.ds(0, NY), 1 - c], b_in, me.at(dc=1))
    for e in (2, 1, 3, 0):
        rows = dot(shuffle, rows_p[:, e * 16:(e + 1) * 16, :].reshape(256, D), ((0,), (0,)))
        arr[e] = rows.astype(BF16).reshape(NZ, 32, D)
    returns = [[] for _ in range(NZ)]
    for i in (4, 3, -3, 2, -2, 1, -1, 0):
        t = (z + i) % NZ
        for e in (2, 1, 3):
            dst = ret.at[t, pl.ds((NX - e) * 32, 32)]
            returns[i % NZ].append(cp.start(arr.at[e, t], dst, me.at(dx=e)))
    for i in range(NZ):
        ret[i, 0:32] = arr[0, i]

    def hidden_one(t, carry):
        columns = pl.ds(pl.multiple_of(t * 256, 256), 256)
        weight = wrel[:, :, :, :, columns].reshape(NX * CL, 256)
        hid[:, :, columns] = dot(delta[...], weight, ((1,), (0,))).reshape(NZ, DOC, 256)
        return carry

    lax.fori_loop(0, 4, hidden_one, 0)

    def combine(i):
        t = (z + i) % NZ
        for copy in returns[i % NZ]:
            copy.wait_recv()
        hid[t] = hid[t] + dot(place[t], ret[t], ((0,), (0,)))

    def z_step(h):
        right, left = (z + h) % NZ, (z - h) % NZ
        combine(h)
        combine(-h)
        z_right.wait_recv()
        z_left.wait_recv()
        if h == 3:
            zs_r[2, 0:half] = (hid[right, 0:half] + zr_r[3, 0:half].astype(F32)).astype(BF16)
            zs_r[2, half:DOC] = hid[right, half:DOC].astype(BF16)
            zs_l[2, half:DOC] = (hid[left, half:DOC] + zr_l[3, half:DOC].astype(F32)).astype(BF16)
            zs_l[2, 0:half] = hid[left, 0:half].astype(BF16)
        else:
            zs_r[h - 1] = (hid[right] + zr_r[h].astype(F32)).astype(BF16)
            zs_l[h - 1] = (hid[left] + zr_l[h].astype(F32)).astype(BF16)
        return (
            cp.start(zs_r.at[h - 1], zr_r.at[h - 1], me.at(dz=1)),
            cp.start(zs_l.at[h - 1], zr_l.at[h - 1], me.at(dz=-1)),
        )

    combine(4)
    zs_r[3, 0:half] = hid[opposite, 0:half].astype(BF16)
    zs_l[3, half:DOC] = hid[opposite, half:DOC].astype(BF16)
    a, b = pl.ds(0, half), pl.ds(half, half)
    z_right = cp.start(zs_r.at[3, a], zr_r.at[3, a], me.at(dz=1))
    z_left = cp.start(zs_l.at[3, b], zr_l.at[3, b], me.at(dz=-1))

    b_core.wait_recv()

    def add_block(i, carry):
        rows = pl.ds(pl.multiple_of((i % 4) * 512, 512), 512)
        gb[i // 4, c, rows] = (gb[i // 4, c, rows].astype(F32) + b_in[i // 4, rows].astype(F32)).astype(BF16)
        return carry

    lax.fori_loop(0, 16, add_block, 0)
    top, low = pl.ds(0, 1024), pl.ds(1024, 1024)
    b_right = cp.start(gb.at[far, c, top], by_2.at[top], me.at(dy=1))
    b_left = cp.start(gb.at[far, c, low], by_2.at[low], me.at(dy=-1))

    z_right, z_left = z_step(3)

    c_right.wait_recv()
    c_left.wait_recv()

    def add_c2(i, carry):
        c_y[i] = (gc[y, c, i].astype(F32) + cy_r[0, i].astype(F32) + cy_r[1, i].astype(F32)).astype(BF16)
        return carry

    lax.fori_loop(0, NX, add_c2, 0)
    ct, cl = pl.ds(0, 64), pl.ds(64, 64)
    x_right = cp.start(c_y.at[2, ct], x_2.at[ct], me.at(dx=1))
    x_left = cp.start(c_y.at[2, cl], x_2.at[cl], me.at(dx=-1))

    z_right, z_left = z_step(2)

    b_right.wait_recv()
    b_left.wait_recv()

    def add_b(i, carry):
        rows = pl.ds(pl.multiple_of(i * 512, 512), 512)
        other = pl.ds(pl.multiple_of(i * 512 + 1024, 512), 512)
        by_s[0, rows] = (gb[up, c, rows].astype(F32) + by_2[rows].astype(F32)).astype(BF16)
        by_s[0, other] = gb[up, c, other]
        by_s[1, other] = (gb[down, c, other].astype(F32) + by_2[other].astype(F32)).astype(BF16)
        by_s[1, rows] = gb[down, c, rows]
        return carry

    lax.fori_loop(0, 2, add_b, 0)
    b_right = cp.start(by_s.at[0], by_r.at[0], me.at(dy=1))
    b_left = cp.start(by_s.at[1], by_r.at[1], me.at(dy=-1))

    z_right, z_left = z_step(1)

    x_right.wait_recv()
    x_left.wait_recv()
    x_s[0, ct] = (c_y[1, ct].astype(F32) + x_2[ct].astype(F32)).astype(BF16)
    x_s[0, cl] = c_y[1, cl]
    x_s[1, cl] = (c_y[3, cl].astype(F32) + x_2[cl].astype(F32)).astype(BF16)
    x_s[1, ct] = c_y[3, ct]
    x_right = cp.start(x_s.at[0], x_r.at[0], me.at(dx=1))
    x_left = cp.start(x_s.at[1], x_r.at[1], me.at(dx=-1))

    combine(0)
    x_right.wait_recv()
    x_left.wait_recv()
    o_c[...] = c_y[0].astype(F32) + x_r[0].astype(F32) + x_r[1].astype(F32)
    done_c = pltpu.make_async_copy(o_c, out_c, local.at[6])
    done_c.start()
    b_right.wait_recv()
    b_left.wait_recv()

    def add_b2(i, carry):
        rows = pl.ds(pl.multiple_of(i * 512, 512), 512)
        o_b[rows] = gb[y, c, rows].astype(F32) + by_r[0, rows].astype(F32) + by_r[1, rows].astype(F32)
        return carry

    lax.fori_loop(0, 4, add_b2, 0)
    done_b = pltpu.make_async_copy(o_b, out_b, local.at[7])
    done_b.start()
    z_right.wait_recv()
    z_left.wait_recv()
    o_h[...] = (hid[z] + zr_r[0].astype(F32) + zr_l[0].astype(F32)).astype(BF16)
    done_h = pltpu.make_async_copy(o_h, out_h, local.at[8])
    done_h.start()
    for copy in (done_c, done_b, done_h):
        copy.wait()
    cp.finish()


def w_part(wrel, group, y, c, part):
    return wrel.at[group, y, c, pl.ds(part * 32, 32)]


def per_device(encoded, positive_clusters, cluster_weight, shortlist, positive_offsets, block_weight):
    vmem = pl.BlockSpec(memory_space=pltpu.VMEM)
    hbm = pl.BlockSpec(memory_space=pl.ANY)
    bf = lambda *shape: pltpu.VMEM(shape, BF16)
    f32 = lambda *shape: pltpu.VMEM(shape, F32)
    copies = 112
    out_h, out_c, out_b = pl.pallas_call(
        kernel,
        out_shape=(
            jax.ShapeDtypeStruct((DOC, D), BF16),
            jax.ShapeDtypeStruct((128, CL), F32),
            jax.ShapeDtypeStruct((2048, 128), F32),
        ),
        in_specs=[hbm] * 6,
        out_specs=(hbm,) * 3,
        scratch_shapes=[
            bf(NZ, DOC, D), bf(D, NZ * DOC), bf(NX, NY, NC, 64, D), bf(16, LBL, D),
            pltpu.VMEM((NZ, 16, 128), jnp.int32), f32(NZ * DOC, 16), bf(NX, NZ, 32, D), f32(NX, NZ, 128),
            f32(16, 64), bf(NZ, 128, 128), bf(NZ, 128, D), bf(16, 64, D), bf(NZ * DOC, NX * CL),
            bf(NZ, 128, D), f32(NZ, DOC, D), bf(4, DOC, D), bf(4, DOC, D), bf(4, DOC, D), bf(4, DOC, D),
            bf(NY, NC, NX, 128, CL), bf(NY, NX, 128, CL), bf(NX, 128, CL), bf(2, NX, 128, CL), bf(2, NX, 128, CL),
            bf(NX, 128, CL), bf(128, CL), bf(2, 128, CL), bf(2, 128, CL),
            bf(NY, NC, 2048, 128), bf(NY, 2048, 128), bf(2048, 128), bf(2, 2048, 128), bf(2, 2048, 128),
            bf(DOC, D), f32(128, CL), f32(2048, 128),
            pltpu.SemaphoreType.DMA((copies,)),
            pltpu.SemaphoreType.DMA((copies,)),
            pltpu.SemaphoreType.DMA((9,)),
        ],
        compiler_params=pltpu.CompilerParams(
            collective_id=0, has_side_effects=True, vmem_limit_bytes=VMEM_LIMIT
        ),
    )(
        encoded, cluster_weight.reshape(NY, NC, 64, D), positive_clusters.T, shortlist.T,
        positive_offsets.T, block_weight,
    )
    out_h, out_c, out_b = pl.pallas_call(
        place_kernel,
        out_shape=(
            jax.ShapeDtypeStruct((DOC, D), BF16),
            jax.ShapeDtypeStruct((CL, 128), F32),
            jax.ShapeDtypeStruct((2048, 128), F32),
        ),
        in_specs=[vmem] * 3,
        out_specs=(vmem,) * 3,
    )(out_h, out_c, out_b)
    return out_h, out_c, out_b.reshape(16, LBL, 128)


def place_kernel(in_h, in_c, in_b, out_h, out_c, out_b):
    out_h[...] = in_h[...]
    out_c[...] = jnp.transpose(in_c[...], (1, 0))
    out_b[...] = in_b[...]


def solution(mesh):
    placed = (
        P(("dp", "label"), None),
        P(("dp", "label"), None),
        P("label", None),
        P(("dp", "label"), None),
        P(("dp", "label"), None),
        P("label", None, None),
    )
    return jax.shard_map(
        per_device,
        mesh=mesh,
        in_specs=placed,
        out_specs=(P(("dp", "label"), None), P("label", "dp"), P("label", None, "dp")),
        check_vma=False,
    )
```

```python
import math

import jax
import jax.numpy as jnp
from jax import lax
from jax.experimental import pallas as pl
from jax.experimental.pallas import tpu as pltpu
from jax.sharding import PartitionSpec as P

MESH = pl.DeviceIdType.MESH
F32, BF16 = jnp.float32, jnp.bfloat16
NY, NC, NX, NZ = 4, 2, 4, 8
DOC, D, CL, LBL = 128, 1024, 512, 128
VMEM_LIMIT = 60 * 1024 * 1024


class Spot:
    def __init__(self):
        dp, label = lax.axis_index("dp"), lax.axis_index("label")
        self.y, self.c = dp // NC, dp % NC
        self.x, self.z = label // NZ, label % NZ

    def at(self, dx=0, dy=0, dz=0, dc=0):
        y, x, z = (self.y + dy) % NY, (self.x + dx) % NX, (self.z + dz) % NZ
        return (y * NC + (self.c + dc) % NC, x * NZ + z)


class Copies:
    def __init__(self, send, recv):
        self.send, self.recv, self.used, self.sent = send, recv, 0, []

    def start(self, src, dst, device):
        i = self.used
        self.used += 1
        copy = pltpu.make_async_remote_copy(
            src_ref=src, dst_ref=dst, send_sem=self.send.at[i], recv_sem=self.recv.at[i],
            device_id=device, device_id_type=MESH,
        )
        copy.start()
        self.sent.append(copy)
        return copy

    def finish(self):
        for copy in self.sent:
            copy.wait_send()


class Chain:
    def __init__(self, cp, side, own, two, s, r, rows=0):
        self.cp, self.side, self.own, self.two, self.s, self.r, self.rows = cp, side, own, two, s, r, rows

    def piece(self, j):
        return pl.ds(j * self.rows, self.rows) if self.rows else j

    def pair(self, j):
        return pl.ds(j * (self.rows or 1), 2 * (self.rows or 1))

    def begin(self):
        a, b = self.pair(0), self.pair(2)
        self.moving = [
            self.cp.start(self.own(2, a), self.two.at[a], self.side(1)),
            self.cp.start(self.own(2, b), self.two.at[b], self.side(-1)),
        ]

    def arrive(self):
        for copy in self.moving:
            copy.wait_recv()

    def middle(self):
        self.arrive()
        for j in range(4):
            at = self.piece(j)
            self.s[j // 2, at] = (self.own(1 + j // 2 * 2, at)[...].astype(F32) + self.two[at].astype(F32)).astype(BF16)
            self.s[1 - j // 2, at] = self.own(3 - j // 2 * 2, at)[...]
        self.moving = [
            self.cp.start(self.s.at[0], self.r.at[0], self.side(1)),
            self.cp.start(self.s.at[1], self.r.at[1], self.side(-1)),
        ]

    def end(self, put):
        self.arrive()
        for j in range(4):
            at = self.piece(j)
            put(at, self.own(0, at)[...].astype(F32) + self.r[0, at].astype(F32) + self.r[1, at].astype(F32))


def dot(a, b, dims):
    return lax.dot_general(a, b, (dims, ((), ())), preferred_element_type=F32)


def sigmoid(v):
    return 0.5 * jnp.tanh(0.5 * v) + 0.5


def iota(shape, dim):
    return lax.broadcasted_iota(jnp.int32, shape, dim)


def kernel(
    enc, w, pos, listed, offsets, bw_hbm, out_h, out_c, out_b,
    docs, docs_t, wrel, bw, metas, pos_t, arr, tgt, off, place, disp, rows_p, delta,
    ret, hid, zs_r, zs_l, zr_r, zr_l,
    gc, c_in, fa_2, fa_s, fa_r, fb_2, fb_s, fb_r, c_a, c_b, ga_2, ga_s, ga_r, gb_2, gb_s, gb_r,
    gb, b_in, by_2, by_s, by_r, o_h, o_c, o_b, send, recv, local,
):
    me = Spot()
    x, y, z, c = me.x, me.y, me.z, me.c
    scale = 1.0 / math.sqrt(DOC * NY * NC * NX * NZ)
    own = [
        pltpu.make_async_copy(enc, docs.at[z], local.at[0]),
        pltpu.make_async_copy(pos, metas.at[z, pl.ds(0, 4)], local.at[1]),
        pltpu.make_async_copy(listed, metas.at[z, pl.ds(4, 4)], local.at[2]),
        pltpu.make_async_copy(offsets, metas.at[z, pl.ds(8, 4)], local.at[3]),
        pltpu.make_async_copy(w, wrel.at[0], local.at[4]),
        pltpu.make_async_copy(bw_hbm, bw, local.at[5]),
    ]
    for copy in own:
        copy.start()
    metas[z, 12:16] = jnp.zeros((4, 128), jnp.int32)
    others = (
        [me.at(dz=i) for i in range(1, NZ)] + [me.at(dx=i) for i in range(1, NX)]
        + [me.at(dy=1), me.at(dy=-1), me.at(dc=1)]
    )
    barrier = pltpu.get_barrier_semaphore()
    for other in others:
        pl.semaphore_signal(barrier, inc=1, device_id=other, device_id_type=MESH)
    cp = Copies(send, recv)
    half = DOC // 2

    slot = iota((128, 128), 0)
    lane = iota((128, 128), 1)
    block = (((x + (slot >> 5)) & 3) * NZ + z) * 16 + (slot & 15)
    turn = ((slot >> 4) & 1).astype(F32)
    upper = jnp.where(slot < lane, 1.0, 0.0).astype(BF16)
    eye = jnp.where(slot == lane, 1.0, 0.0).astype(BF16)
    row8 = iota((8, 128), 0)
    tgt[0] = jnp.zeros((8, 128), F32)
    arrivals = [[] for _ in range(NX)]

    def choose(zs):
        info = metas[zs]
        named = jnp.zeros((128, 128), F32)
        offset = jnp.zeros((128, 128), F32)
        for k in range(4):
            hit = info[4 + k:5 + k, :] == block
            named = jnp.where(hit, 1.0, named)
            offset = jnp.where(hit, (info[8 + k:9 + k, :] + 1).astype(F32), offset)
        rank = dot(named.astype(BF16), upper, ((1,), (0,)))
        chosen = jnp.where(rank == turn, named, 0.0)
        place[zs] = chosen.astype(BF16)
        disp[zs] = dot(chosen.astype(BF16), docs[zs], ((1,), (0,))).astype(BF16)
        pick = jnp.where(row8 == zs, 1.0, 0.0).astype(BF16)
        tgt[0] += dot(pick, (chosen * offset).astype(BF16), ((1,), (1,)))

    def hand_on(zs):
        for d in (2, 1, 3):
            arrivals[NX - d].append(
                cp.start(disp.at[zs, pl.ds(d * 32, 32)], arr.at[NX - d, zs], me.at(dx=d))
            )
        arr[0, zs] = disp[zs, 0:32]

    def dispatch(zs):
        choose(zs)
        hand_on(zs)

    def prepare(zs):
        columns = pl.ds(pl.multiple_of(zs * 128, 128), 128)
        for j in range(D // 128):
            docs_t[pl.ds(j * 128, 128), columns] = dot(
                eye, docs[zs, :, j * 128:(j + 1) * 128], ((1,), (1,))
            ).astype(BF16)
        pos_t[columns, :] = jnp.transpose(metas[zs].astype(F32), (1, 0))

    def first(tile, pos, base):
        ids = (base + iota((1, tile.shape[1]), 1)).astype(F32)
        hit = pos[:, 0:1] == ids
        for k in range(1, 4):
            hit = hit | (pos[:, k:k + 1] == ids)
        return (sigmoid(tile) - jnp.where(hit, 1.0, 0.0)).astype(BF16)

    def own_group(zs):
        rows = pl.ds(pl.multiple_of(zs * 128, 128), 128)
        tile = dot(docs[zs], wrel[0].reshape(CL, D), ((1,), (1,)))
        delta[rows, 0:CL] = first(tile, pos_t[rows, :], (x * NZ + z) * CL)

    for i in range(4):
        own[i].wait()
    choose(z)
    prepare(z)
    pl.semaphore_wait(barrier, len(others))
    halves = (pl.ds(0, half), pl.ds(half, half))

    def pass_on(zs, part, dz):
        return cp.start(docs.at[zs, halves[part]], docs.at[zs, halves[part]], me.at(dz=dz))

    right, left = [None, None], [None, None]
    for part in range(2):
        right[part] = pass_on(z, part, 1)
        left[1 - part] = pass_on(z, 1 - part, -1)
    w_right = cp.start(w.at[y, c], wrel.at[3, y, c], me.at(dx=1))
    w_left = cp.start(w.at[y, c], wrel.at[1, y, c], me.at(dx=-1))
    got_meta = [None] + [cp.start(metas.at[z], metas.at[z], me.at(dz=i)) for i in range(1, NZ)]
    own[4].wait()
    own_group(z)
    groups = pl.ds(1, 3)
    w_right.wait_recv()
    w_left.wait_recv()
    w_right = cp.start(w_part(wrel, 3, y, c, 0), w_part(wrel, 2, y, c, 0), me.at(dx=1))
    w_left = cp.start(w_part(wrel, 1, y, c, 1), w_part(wrel, 2, y, c, 1), me.at(dx=-1))
    hand_on(z)
    for h in range(1, NZ // 2):
        from_left, from_right = (z - h) % NZ, (z + h) % NZ
        for part in range(2):
            right[part].wait_recv()
            if h + 1 < NZ // 2 or part == 0:
                right[part] = pass_on(from_left, part, 1)
            left[1 - part].wait_recv()
            if h + 1 < NZ // 2 or part == 0:
                left[1 - part] = pass_on(from_right, 1 - part, -1)
        if h == 1:
            w_right.wait_recv()
            w_left.wait_recv()
            y_right = cp.start(wrel.at[groups, y, c], wrel.at[groups, y, c], me.at(dy=1))
            y_left = cp.start(wrel.at[groups, y, c], wrel.at[groups, y, c], me.at(dy=-1))
            sib = [cp.start(wrel.at[groups, y, c], wrel.at[groups, y, c], me.at(dc=1))]
        got_meta[h].wait_recv()
        dispatch(from_left)
        got_meta[NZ - h].wait_recv()
        dispatch(from_right)
        if h == 3:
            y_right.wait_recv()
            y_left.wait_recv()
            yl, yr = (y - 1) % NY, (y + 1) % NY
            a, b = pl.ds(0, 32), pl.ds(32, 32)
            y_right = cp.start(wrel.at[groups, yl, c, a], wrel.at[groups, yl, c, a], me.at(dy=1))
            y_left = cp.start(wrel.at[groups, yr, c, b], wrel.at[groups, yr, c, b], me.at(dy=-1))
            sib.append(cp.start(wrel.at[groups, yl, c], wrel.at[groups, yl, c], me.at(dc=1)))
            sib.append(cp.start(wrel.at[groups, yr, c], wrel.at[groups, yr, c], me.at(dc=1)))
        for zs in (from_left, from_right):
            prepare(zs)
            own_group(zs)
    right[0].wait_recv()
    left[1].wait_recv()
    got_meta[NZ // 2].wait_recv()
    opposite = (z + NZ // 2) % NZ
    dispatch(opposite)
    for d in range(1, NX):
        arrivals[NX - d].append(cp.start(tgt.at[0], tgt.at[NX - d], me.at(dx=d)))
    prepare(opposite)
    own_group(opposite)

    def scores_one(copies, yi):
        for copy in copies:
            copy.wait_recv()
        weight = wrel[1:NX, yi].reshape(3 * 128, D)
        tile = dot(docs[...].reshape(NZ * DOC, D), weight, ((1,), (1,)))
        for g in range(1, NX):
            base = (((x + g) % NX) * NZ + z) * CL + yi * 128
            columns = pl.ds(pl.multiple_of(g * CL + yi * 128, 128), 128)
            delta[:, columns] = first(tile[:, (g - 1) * 128:g * 128], pos_t[...], base)

    scores_one(sib[0:1], y)
    scores_one(sib[1:2], yl)
    y_right.wait_recv()
    y_left.wait_recv()
    far = (y + 2) % NY
    sib.append(cp.start(wrel.at[groups, far, c], wrel.at[groups, far, c], me.at(dc=1)))
    scores_one(sib[2:3], yr)

    to, fro = iota((256, 256), 0), iota((256, 256), 1)
    moved = ((to >> 1) & 7) * 32 + (to & 1) * 16 + (to >> 4)
    shuffle = jnp.where(fro == moved, 1.0, 0.0).astype(BF16)
    offs = jnp.zeros((16, 64), F32)
    for e in range(NX):
        for copy in arrivals[e]:
            copy.wait_recv()
        rows = dot(shuffle, arr[e].reshape(256, D), ((1,), (0,))).astype(BF16)
        rows_p[:, e * 16:(e + 1) * 16, :] = rows.reshape(16, 16, D)
        for t in range(2):
            at = ((NX - e) % NX) * 32 + t * 16
            take = jnp.where(iota((16, 128), 1) == iota((16, 128), 0) + at, 1.0, 0.0).astype(BF16)
            put = jnp.where(iota((8, 64), 1) == iota((8, 64), 0) * 2 + (e * 16 + t), 1.0, 0.0).astype(BF16)
            taken = dot(take, tgt[e].astype(BF16), ((1,), (1,))).astype(BF16)
            offs = offs + dot(taken, put, ((1,), (0,)))
    off[...] = offs
    own[5].wait()

    def second(i, carry):
        pair = (2 * i, 2 * i + 1)
        scores = [dot(bw[b], rows_p[b], ((1,), (1,))) for b in pair]
        dts = []
        for b, score in zip(pair, scores):
            wanted = off[pl.ds(b, 1), :]
            target = jnp.where(iota((LBL, 64), 0).astype(F32) + 1.0 == wanted, 1.0, 0.0)
            dts.append(jnp.where(wanted > 0.0, sigmoid(score) - target, 0.0).astype(BF16))
        grads = [dot(dt, rows_p[b], ((1,), (0,))) for b, dt in zip(pair, dts)]
        backs = [dot(dt, bw[b], ((0,), (0,))) for b, dt in zip(pair, dts)]
        for b, grad, value in zip(pair, grads, backs):
            at = pl.ds(pl.multiple_of(b * LBL, LBL), LBL)
            grad = (grad * scale).astype(BF16)
            for j in range(NY * NC):
                gb[j // NC, j % NC, at, :] = grad[:, j * 128:(j + 1) * 128]
            rows_p[b] = value.astype(BF16)
        return carry

    b_core = []
    for i in range(2):
        lax.fori_loop(4 * i, 4 * i + 4, second, 0)
        rows = pl.ds(1024 * i, 1024)
        b_core.append(
            cp.start(gb.at[pl.ds(0, NY), 1 - c, rows], b_in.at[pl.ds(0, NY), rows], me.at(dc=1))
        )
    for e in (2, 1, 3, 0):
        rows = dot(shuffle, rows_p[:, e * 16:(e + 1) * 16, :].reshape(256, D), ((0,), (0,)))
        arr[e] = rows.astype(BF16).reshape(NZ, 32, D)
    returns = [[] for _ in range(NZ)]
    for i in (4, 3, -3, 2, -2, 1, -1, 0):
        t = (z + i) % NZ
        for e in (2, 1, 3):
            dst = ret.at[t, pl.ds((NX - e) * 32, 32)]
            returns[i % NZ].append(cp.start(arr.at[e, t], dst, me.at(dx=e)))
    for i in range(NZ):
        ret[i, 0:32] = arr[0, i]

    def grad_one(t, carry):
        columns = pl.ds(pl.multiple_of(t * 256, 256), 256)
        grad = dot(docs_t[...], delta[:, columns], ((1,), (0,))) * scale
        at = pl.ds(pl.multiple_of((t % 2) * 256, 256), 256)
        gc[:, :, t // 2, :, at] = grad.astype(BF16).reshape(NY, NC, 128, 256)
        return carry

    scores_one(sib[3:4], far)
    c_core = []
    for g in range(NX):
        lax.fori_loop(2 * g, 2 * g + 2, grad_one, 0)
        c_core.append(
            cp.start(gc.at[pl.ds(0, NY), 1 - c, g], c_in.at[pl.ds(0, NY), g], me.at(dc=1))
        )

    along_x, along_y = (lambda i: me.at(dx=i)), (lambda i: me.at(dy=i))
    a_rows, b_rows = pl.ds(0, 64), pl.ds(64, 64)
    blocks = Chain(cp, along_y, lambda k, at: gb.at[(y + k) % NY, c, at], by_2, by_s, by_r, 512)
    first_a = Chain(cp, along_y, lambda k, at: gc.at[(y + k) % NY, c, at, a_rows], fa_2, fa_s, fa_r)
    first_b = Chain(cp, along_x, lambda k, at: gc.at[at, c, k, b_rows], fb_2, fb_s, fb_r)
    then_a = Chain(cp, along_x, lambda k, at: c_a.at[k, at], ga_2, ga_s, ga_r, 16)
    then_b = Chain(cp, along_y, lambda k, at: c_b.at[(y + k) % NY, at], gb_2, gb_s, gb_r, 16)

    for copy in b_core:
        copy.wait_recv()

    def add_block(i, carry):
        rows = pl.ds(pl.multiple_of((i % 4) * 512, 512), 512)
        gb[i // 4, c, rows] = (gb[i // 4, c, rows].astype(F32) + b_in[i // 4, rows].astype(F32)).astype(BF16)
        return carry

    lax.fori_loop(0, 16, add_block, 0)
    blocks.begin()

    def hidden_one(t, carry):
        columns = pl.ds(pl.multiple_of(t * 256, 256), 256)
        weight = wrel[:, :, :, :, columns].reshape(NX * CL, 256)
        hid[:, :, columns] = dot(delta[...], weight, ((1,), (0,))).reshape(NZ, DOC, 256)
        return carry

    lax.fori_loop(0, 2, hidden_one, 0)
    for copy in c_core:
        copy.wait_recv()

    def add_cluster(i, carry):
        t, g = i // 4, i % 4
        gc[t, c, g] = (gc[t, c, g].astype(F32) + c_in[t, g].astype(F32)).astype(BF16)
        return carry

    lax.fori_loop(0, 16, add_cluster, 0)
    first_a.begin()
    first_b.begin()
    lax.fori_loop(2, 4, hidden_one, 0)

    def combine(i):
        t = (z + i) % NZ
        for copy in returns[i % NZ]:
            copy.wait_recv()
        hid[t] = hid[t] + dot(place[t], ret[t], ((0,), (0,)))

    z_right, z_left = [None, None], [None, None]
    parts = (slice(0, D // 2), slice(D // 2, D))

    def z_send(h, p):
        z_right[p] = cp.start(zs_r.at[h - 1, p], zr_r.at[h - 1, p], me.at(dz=1))
        z_left[p] = cp.start(zs_l.at[h - 1, p], zr_l.at[h - 1, p], me.at(dz=-1))

    def z_step(h):
        right, left = (z + h) % NZ, (z - h) % NZ
        combine(h)
        combine(-h)
        for p, cols in enumerate(parts):
            z_right[p].wait_recv()
            z_left[p].wait_recv()
            if h == 3:
                zs_r[2, p, 0:half] = (hid[right, 0:half, cols] + zr_r[3, p, 0:half].astype(F32)).astype(BF16)
                zs_r[2, p, half:DOC] = hid[right, half:DOC, cols].astype(BF16)
                zs_l[2, p, half:DOC] = (hid[left, half:DOC, cols] + zr_l[3, p, half:DOC].astype(F32)).astype(BF16)
                zs_l[2, p, 0:half] = hid[left, 0:half, cols].astype(BF16)
            else:
                zs_r[h - 1, p] = (hid[right, :, cols] + zr_r[h, p].astype(F32)).astype(BF16)
                zs_l[h - 1, p] = (hid[left, :, cols] + zr_l[h, p].astype(F32)).astype(BF16)
            z_send(h, p)

    combine(4)
    for p, cols in enumerate(parts):
        zs_r[3, p, 0:half] = hid[opposite, 0:half, cols].astype(BF16)
        zs_l[3, p, half:DOC] = hid[opposite, half:DOC, cols].astype(BF16)
        z_right[p] = cp.start(zs_r.at[3, p, halves[0]], zr_r.at[3, p, halves[0]], me.at(dz=1))
        z_left[p] = cp.start(zs_l.at[3, p, halves[1]], zr_l.at[3, p, halves[1]], me.at(dz=-1))

    def put(ref):
        def store(at, value):
            ref[at] = value.astype(ref.dtype)

        return store

    def put_b(at, value):
        o_c[pl.ds(64 + at.start, at.size)] = value

    blocks.middle()
    z_step(3)
    first_a.middle()
    z_step(2)
    first_b.middle()
    z_step(1)
    blocks.end(put(o_b))
    done_b = pltpu.make_async_copy(o_b, out_b, local.at[7])
    done_b.start()
    combine(0)
    first_b.end(put(c_b))
    then_b.begin()
    first_a.end(put(c_a))
    then_a.begin()
    then_b.middle()
    then_a.middle()
    for p, cols in enumerate(parts):
        z_right[p].wait_recv()
        z_left[p].wait_recv()
        o_h[:, cols] = (hid[z, :, cols] + zr_r[0, p].astype(F32) + zr_l[0, p].astype(F32)).astype(BF16)
    done_h = pltpu.make_async_copy(o_h, out_h, local.at[8])
    done_h.start()
    then_b.end(put_b)
    then_a.end(put(o_c))
    done_c = pltpu.make_async_copy(o_c, out_c, local.at[6])
    done_c.start()
    for copy in (done_c, done_b, done_h):
        copy.wait()
    cp.finish()


def w_part(wrel, group, y, c, part):
    return wrel.at[group, y, c, pl.ds(part * 32, 32)]


def per_device(encoded, positive_clusters, cluster_weight, shortlist, positive_offsets, block_weight):
    vmem = pl.BlockSpec(memory_space=pltpu.VMEM)
    hbm = pl.BlockSpec(memory_space=pl.ANY)
    bf = lambda *shape: pltpu.VMEM(shape, BF16)
    f32 = lambda *shape: pltpu.VMEM(shape, F32)
    copies = 128
    out_h, out_c, out_b = pl.pallas_call(
        kernel,
        out_shape=(
            jax.ShapeDtypeStruct((DOC, D), BF16),
            jax.ShapeDtypeStruct((128, CL), F32),
            jax.ShapeDtypeStruct((2048, 128), F32),
        ),
        in_specs=[hbm] * 6,
        out_specs=(hbm,) * 3,
        scratch_shapes=[
            bf(NZ, DOC, D), bf(D, NZ * DOC), bf(NX, NY, NC, 64, D), bf(16, LBL, D),
            pltpu.VMEM((NZ, 16, 128), jnp.int32), f32(NZ * DOC, 16), bf(NX, NZ, 32, D), f32(NX, NZ, 128),
            f32(16, 64), bf(NZ, 128, 128), bf(NZ, 128, D), bf(16, 64, D), bf(NZ * DOC, NX * CL),
            bf(NZ, 128, D), f32(NZ, DOC, D), bf(4, 2, DOC, D // 2), bf(4, 2, DOC, D // 2), bf(4, 2, DOC, D // 2),
            bf(4, 2, DOC, D // 2),
            bf(NY, NC, NX, 128, CL), bf(NY, NX, 128, CL),
            bf(4, 64, CL), bf(2, 4, 64, CL), bf(2, 4, 64, CL), bf(4, 64, CL), bf(2, 4, 64, CL), bf(2, 4, 64, CL),
            bf(4, 64, CL), bf(4, 64, CL), bf(64, CL), bf(2, 64, CL), bf(2, 64, CL), bf(64, CL), bf(2, 64, CL), bf(2, 64, CL),
            bf(NY, NC, 2048, 128), bf(NY, 2048, 128), bf(2048, 128), bf(2, 2048, 128), bf(2, 2048, 128),
            bf(DOC, D), f32(128, CL), f32(2048, 128),
            pltpu.SemaphoreType.DMA((copies,)),
            pltpu.SemaphoreType.DMA((copies,)),
            pltpu.SemaphoreType.DMA((9,)),
        ],
        compiler_params=pltpu.CompilerParams(
            collective_id=0, has_side_effects=True, vmem_limit_bytes=VMEM_LIMIT
        ),
    )(
        encoded, cluster_weight.reshape(NY, NC, 64, D), positive_clusters.T, shortlist.T,
        positive_offsets.T, block_weight,
    )
    out_h, out_c, out_b = pl.pallas_call(
        place_kernel,
        out_shape=(
            jax.ShapeDtypeStruct((DOC, D), BF16),
            jax.ShapeDtypeStruct((CL, 128), F32),
            jax.ShapeDtypeStruct((2048, 128), F32),
        ),
        in_specs=[vmem] * 3,
        out_specs=(vmem,) * 3,
    )(out_h, out_c, out_b)
    return out_h, out_c, out_b.reshape(16, LBL, 128)


def place_kernel(in_h, in_c, in_b, out_h, out_c, out_b):
    out_h[...] = in_h[...]
    out_c[...] = jnp.transpose(in_c[...], (1, 0))
    out_b[...] = in_b[...]


def solution(mesh):
    placed = (
        P(("dp", "label"), None),
        P(("dp", "label"), None),
        P("label", None),
        P(("dp", "label"), None),
        P(("dp", "label"), None),
        P("label", None, None),
    )
    return jax.shard_map(
        per_device,
        mesh=mesh,
        in_specs=placed,
        out_specs=(P(("dp", "label"), None), P("label", "dp"), P("label", None, "dp")),
        check_vma=False,
    )
```

```python
import math

import jax
import jax.numpy as jnp
from jax import lax
from jax.experimental import pallas as pl
from jax.experimental.pallas import tpu as pltpu
from jax.sharding import PartitionSpec as P

MESH = pl.DeviceIdType.MESH
F32, BF16 = jnp.float32, jnp.bfloat16
NY, NC, NX, NZ = 4, 2, 4, 8
DOC, D, CL, LBL = 128, 1024, 512, 128
VMEM_LIMIT = 60 * 1024 * 1024


class Spot:
    def __init__(self):
        dp, label = lax.axis_index("dp"), lax.axis_index("label")
        self.y, self.c = dp // NC, dp % NC
        self.x, self.z = label // NZ, label % NZ

    def at(self, dx=0, dy=0, dz=0, dc=0):
        y, x, z = (self.y + dy) % NY, (self.x + dx) % NX, (self.z + dz) % NZ
        return (y * NC + (self.c + dc) % NC, x * NZ + z)


class Copies:
    def __init__(self, send, recv):
        self.send, self.recv, self.used, self.sent = send, recv, 0, []

    def start(self, src, dst, device):
        i = self.used
        self.used += 1
        copy = pltpu.make_async_remote_copy(
            src_ref=src, dst_ref=dst, send_sem=self.send.at[i], recv_sem=self.recv.at[i],
            device_id=device, device_id_type=MESH,
        )
        copy.start()
        self.sent.append(copy)
        return copy

    def finish(self):
        for copy in self.sent:
            copy.wait_send()


class Chain:
    def __init__(self, cp, side, own, two, s, r, rows=0):
        self.cp, self.side, self.own, self.two, self.s, self.r, self.rows = cp, side, own, two, s, r, rows

    def piece(self, j):
        return pl.ds(j * self.rows, self.rows) if self.rows else j

    def pair(self, j):
        return pl.ds(j * (self.rows or 1), 2 * (self.rows or 1))

    def begin(self):
        a, b = self.pair(0), self.pair(2)
        self.moving = [
            self.cp.start(self.own(2, a), self.two.at[a], self.side(1)),
            self.cp.start(self.own(2, b), self.two.at[b], self.side(-1)),
        ]

    def arrive(self):
        for copy in self.moving:
            copy.wait_recv()

    def middle(self):
        self.arrive()
        for j in range(4):
            at = self.piece(j)
            self.s[j // 2, at] = (self.own(1 + j // 2 * 2, at)[...].astype(F32) + self.two[at].astype(F32)).astype(BF16)
            self.s[1 - j // 2, at] = self.own(3 - j // 2 * 2, at)[...]
        self.moving = [
            self.cp.start(self.s.at[0], self.r.at[0], self.side(1)),
            self.cp.start(self.s.at[1], self.r.at[1], self.side(-1)),
        ]

    def end(self, put):
        self.arrive()
        for j in range(4):
            at = self.piece(j)
            put(at, self.own(0, at)[...].astype(F32) + self.r[0, at].astype(F32) + self.r[1, at].astype(F32))


def dot(a, b, dims):
    return lax.dot_general(a, b, (dims, ((), ())), preferred_element_type=F32)


def sigmoid(v):
    return 0.5 * jnp.tanh(0.5 * v) + 0.5


def iota(shape, dim):
    return lax.broadcasted_iota(jnp.int32, shape, dim)


def kernel(
    enc, w, pos, listed, offsets, bw_hbm, out_h, out_c, out_b,
    docs, docs_t, wrel, bw, metas, pos_t, arr, tgt, off, place, disp, rows_p, delta,
    ret, hid, zs_r, zs_l, zr_r, zr_l,
    gc, c_in, fa_2, fa_s, fa_r, fb_2, fb_s, fb_r, c_a, c_b, ga_2, ga_s, ga_r, gb_2, gb_s, gb_r,
    gb, b_in, by_2, by_s, by_r, o_h, o_c, o_b, send, recv, local,
):
    me = Spot()
    x, y, z, c = me.x, me.y, me.z, me.c
    scale = 1.0 / math.sqrt(DOC * NY * NC * NX * NZ)
    own = [
        pltpu.make_async_copy(enc, docs.at[z], local.at[0]),
        pltpu.make_async_copy(pos, metas.at[z, pl.ds(0, 4)], local.at[1]),
        pltpu.make_async_copy(listed, metas.at[z, pl.ds(4, 4)], local.at[2]),
        pltpu.make_async_copy(offsets, metas.at[z, pl.ds(8, 4)], local.at[3]),
        pltpu.make_async_copy(w, wrel.at[0], local.at[4]),
        pltpu.make_async_copy(bw_hbm, bw, local.at[5]),
    ]
    for copy in own:
        copy.start()
    metas[z, 12:16] = jnp.zeros((4, 128), jnp.int32)
    others = (
        [me.at(dz=i) for i in range(1, NZ)] + [me.at(dx=i) for i in range(1, NX)]
        + [me.at(dy=1), me.at(dy=-1), me.at(dc=1)]
    )
    barrier = pltpu.get_barrier_semaphore()
    for other in others:
        pl.semaphore_signal(barrier, inc=1, device_id=other, device_id_type=MESH)
    cp = Copies(send, recv)
    half = DOC // 2

    slot = iota((128, 128), 0)
    lane = iota((128, 128), 1)
    block = (((x + (slot >> 5)) & 3) * NZ + z) * 16 + (slot & 15)
    turn = ((slot >> 4) & 1).astype(F32)
    upper = jnp.where(slot < lane, 1.0, 0.0).astype(BF16)
    eye = jnp.where(slot == lane, 1.0, 0.0).astype(BF16)
    row8 = iota((8, 128), 0)
    tgt[0] = jnp.zeros((8, 128), F32)
    arrivals = [[] for _ in range(NX)]

    def choose(zs):
        info = metas[zs]
        named = jnp.zeros((128, 128), F32)
        offset = jnp.zeros((128, 128), F32)
        for k in range(4):
            hit = info[4 + k:5 + k, :] == block
            named = jnp.where(hit, 1.0, named)
            offset = jnp.where(hit, (info[8 + k:9 + k, :] + 1).astype(F32), offset)
        rank = dot(named.astype(BF16), upper, ((1,), (0,)))
        chosen = jnp.where(rank == turn, named, 0.0)
        place[zs] = chosen.astype(BF16)
        disp[zs] = dot(chosen.astype(BF16), docs[zs], ((1,), (0,))).astype(BF16)
        pick = jnp.where(row8 == zs, 1.0, 0.0).astype(BF16)
        tgt[0] += dot(pick, (chosen * offset).astype(BF16), ((1,), (1,)))

    def hand_on(zs):
        for d in (2, 1, 3):
            arrivals[NX - d].append(
                cp.start(disp.at[zs, pl.ds(d * 32, 32)], arr.at[NX - d, zs], me.at(dx=d))
            )
        arr[0, zs] = disp[zs, 0:32]

    def dispatch(zs):
        choose(zs)
        hand_on(zs)

    def prepare(zs):
        columns = pl.ds(pl.multiple_of(zs * 128, 128), 128)
        for j in range(D // 128):
            docs_t[pl.ds(j * 128, 128), columns] = dot(
                eye, docs[zs, :, j * 128:(j + 1) * 128], ((1,), (1,))
            ).astype(BF16)
        pos_t[columns, :] = jnp.transpose(metas[zs].astype(F32), (1, 0))

    def first(tile, pos, base):
        ids = (base + iota((1, tile.shape[1]), 1)).astype(F32)
        hit = pos[:, 0:1] == ids
        for k in range(1, 4):
            hit = hit | (pos[:, k:k + 1] == ids)
        return (sigmoid(tile) - jnp.where(hit, 1.0, 0.0)).astype(BF16)

    def own_group(zs):
        rows = pl.ds(pl.multiple_of(zs * 128, 128), 128)
        tile = dot(docs[zs], wrel[0].reshape(CL, D), ((1,), (1,)))
        delta[rows, 0:CL] = first(tile, pos_t[rows, :], (x * NZ + z) * CL)

    for i in range(4):
        own[i].wait()
    choose(z)
    prepare(z)
    pl.semaphore_wait(barrier, len(others))
    halves = (pl.ds(0, half), pl.ds(half, half))

    def pass_on(zs, part, dz):
        return cp.start(docs.at[zs, halves[part]], docs.at[zs, halves[part]], me.at(dz=dz))

    right, left = [None, None], [None, None]
    for part in range(2):
        right[part] = pass_on(z, part, 1)
        left[1 - part] = pass_on(z, 1 - part, -1)
    w_right = cp.start(w.at[y, c], wrel.at[3, y, c], me.at(dx=1))
    w_left = cp.start(w.at[y, c], wrel.at[1, y, c], me.at(dx=-1))
    got_meta = [None] + [cp.start(metas.at[z], metas.at[z], me.at(dz=i)) for i in range(1, NZ)]
    own[4].wait()
    own_group(z)
    groups = pl.ds(1, 3)
    w_right.wait_recv()
    w_left.wait_recv()
    w_right = cp.start(w_part(wrel, 3, y, c, 0), w_part(wrel, 2, y, c, 0), me.at(dx=1))
    w_left = cp.start(w_part(wrel, 1, y, c, 1), w_part(wrel, 2, y, c, 1), me.at(dx=-1))
    hand_on(z)
    for h in range(1, NZ // 2):
        from_left, from_right = (z - h) % NZ, (z + h) % NZ
        for part in range(2):
            right[part].wait_recv()
            if h + 1 < NZ // 2 or part == 0:
                right[part] = pass_on(from_left, part, 1)
            left[1 - part].wait_recv()
            if h + 1 < NZ // 2 or part == 0:
                left[1 - part] = pass_on(from_right, 1 - part, -1)
        if h == 1:
            w_right.wait_recv()
            w_left.wait_recv()
            y_right = cp.start(wrel.at[groups, y, c], wrel.at[groups, y, c], me.at(dy=1))
            y_left = cp.start(wrel.at[groups, y, c], wrel.at[groups, y, c], me.at(dy=-1))
            sib = [cp.start(wrel.at[groups, y, c], wrel.at[groups, y, c], me.at(dc=1))]
        got_meta[h].wait_recv()
        dispatch(from_left)
        got_meta[NZ - h].wait_recv()
        dispatch(from_right)
        if h == 3:
            y_right.wait_recv()
            y_left.wait_recv()
            yl, yr = (y - 1) % NY, (y + 1) % NY
            a, b = pl.ds(0, 32), pl.ds(32, 32)
            y_right = cp.start(wrel.at[groups, yl, c, a], wrel.at[groups, yl, c, a], me.at(dy=1))
            y_left = cp.start(wrel.at[groups, yr, c, b], wrel.at[groups, yr, c, b], me.at(dy=-1))
            sib.append(cp.start(wrel.at[groups, yl, c], wrel.at[groups, yl, c], me.at(dc=1)))
            sib.append(cp.start(wrel.at[groups, yr, c], wrel.at[groups, yr, c], me.at(dc=1)))
        for zs in (from_left, from_right):
            prepare(zs)
            own_group(zs)
    right[0].wait_recv()
    left[1].wait_recv()
    got_meta[NZ // 2].wait_recv()
    opposite = (z + NZ // 2) % NZ
    dispatch(opposite)
    for d in range(1, NX):
        arrivals[NX - d].append(cp.start(tgt.at[0], tgt.at[NX - d], me.at(dx=d)))
    prepare(opposite)
    own_group(opposite)

    def scores_one(copies, yi):
        for copy in copies:
            copy.wait_recv()
        weight = wrel[1:NX, yi].reshape(3 * 128, D)
        tile = dot(docs[...].reshape(NZ * DOC, D), weight, ((1,), (1,)))
        for g in range(1, NX):
            base = (((x + g) % NX) * NZ + z) * CL + yi * 128
            columns = pl.ds(pl.multiple_of(g * CL + yi * 128, 128), 128)
            delta[:, columns] = first(tile[:, (g - 1) * 128:g * 128], pos_t[...], base)

    scores_one(sib[0:1], y)
    scores_one(sib[1:2], yl)
    y_right.wait_recv()
    y_left.wait_recv()
    far = (y + 2) % NY
    sib.append(cp.start(wrel.at[groups, far, c], wrel.at[groups, far, c], me.at(dc=1)))
    scores_one(sib[2:3], yr)

    to, fro = iota((256, 256), 0), iota((256, 256), 1)
    moved = ((to >> 1) & 7) * 32 + (to & 1) * 16 + (to >> 4)
    shuffle = jnp.where(fro == moved, 1.0, 0.0).astype(BF16)
    offs = jnp.zeros((16, 64), F32)
    for e in range(NX):
        for copy in arrivals[e]:
            copy.wait_recv()
        rows = dot(shuffle, arr[e].reshape(256, D), ((1,), (0,))).astype(BF16)
        rows_p[:, e * 16:(e + 1) * 16, :] = rows.reshape(16, 16, D)
        for t in range(2):
            at = ((NX - e) % NX) * 32 + t * 16
            take = jnp.where(iota((16, 128), 1) == iota((16, 128), 0) + at, 1.0, 0.0).astype(BF16)
            put = jnp.where(iota((8, 64), 1) == iota((8, 64), 0) * 2 + (e * 16 + t), 1.0, 0.0).astype(BF16)
            taken = dot(take, tgt[e].astype(BF16), ((1,), (1,))).astype(BF16)
            offs = offs + dot(taken, put, ((1,), (0,)))
    off[...] = offs
    own[5].wait()

    def second(i, carry):
        pair = (2 * i, 2 * i + 1)
        scores = [dot(bw[b], rows_p[b], ((1,), (1,))) for b in pair]
        dts = []
        for b, score in zip(pair, scores):
            wanted = off[pl.ds(b, 1), :]
            target = jnp.where(iota((LBL, 64), 0).astype(F32) + 1.0 == wanted, 1.0, 0.0)
            dts.append(jnp.where(wanted > 0.0, sigmoid(score) - target, 0.0).astype(BF16))
        grads = [dot(dt, rows_p[b], ((1,), (0,))) for b, dt in zip(pair, dts)]
        backs = [dot(dt, bw[b], ((0,), (0,))) for b, dt in zip(pair, dts)]
        for b, grad, value in zip(pair, grads, backs):
            at = pl.ds(pl.multiple_of(b * LBL, LBL), LBL)
            grad = (grad * scale).astype(BF16)
            for j in range(NY * NC):
                gb[j // NC, j % NC, at, :] = grad[:, j * 128:(j + 1) * 128]
            rows_p[b] = value.astype(BF16)
        return carry

    b_core = []
    for i in range(2):
        lax.fori_loop(4 * i, 4 * i + 4, second, 0)
        rows = pl.ds(1024 * i, 1024)
        b_core.append(
            cp.start(gb.at[pl.ds(0, NY), 1 - c, rows], b_in.at[pl.ds(0, NY), rows], me.at(dc=1))
        )
    for e in (2, 1, 3, 0):
        rows = dot(shuffle, rows_p[:, e * 16:(e + 1) * 16, :].reshape(256, D), ((0,), (0,)))
        arr[e] = rows.astype(BF16).reshape(NZ, 32, D)
    returns = [[] for _ in range(NZ)]

    def send_back(i):
        t = (z + i) % NZ
        for e in (2, 1, 3):
            dst = ret.at[t, pl.ds((NX - e) * 32, 32)]
            returns[i % NZ].append(cp.start(arr.at[e, t], dst, me.at(dx=e)))

    for i in (4, 3, -3, 2, -2):
        send_back(i)
    for i in range(NZ):
        ret[i, 0:32] = arr[0, i]

    def grad_one(t, carry):
        columns = pl.ds(pl.multiple_of(t * 256, 256), 256)
        grad = dot(docs_t[...], delta[:, columns], ((1,), (0,))) * scale
        at = pl.ds(pl.multiple_of((t % 2) * 256, 256), 256)
        gc[:, :, t // 2, :, at] = grad.astype(BF16).reshape(NY, NC, 128, 256)
        return carry

    along_x, along_y = (lambda i: me.at(dx=i)), (lambda i: me.at(dy=i))
    a_rows, b_rows = pl.ds(0, 64), pl.ds(64, 64)
    blocks = Chain(cp, along_y, lambda k, at: gb.at[(y + k) % NY, c, at], by_2, by_s, by_r, 512)
    first_a = Chain(cp, along_y, lambda k, at: gc.at[(y + k) % NY, c, at, a_rows], fa_2, fa_s, fa_r)
    first_b = Chain(cp, along_x, lambda k, at: gc.at[at, c, k, b_rows], fb_2, fb_s, fb_r)
    then_a = Chain(cp, along_x, lambda k, at: c_a.at[k, at], ga_2, ga_s, ga_r, 16)
    then_b = Chain(cp, along_y, lambda k, at: c_b.at[(y + k) % NY, at], gb_2, gb_s, gb_r, 16)

    scores_one(sib[3:4], far)
    for copy in b_core:
        copy.wait_recv()

    def add_block(i, carry):
        rows = pl.ds(pl.multiple_of((i % 4) * 512, 512), 512)
        gb[i // 4, c, rows] = (gb[i // 4, c, rows].astype(F32) + b_in[i // 4, rows].astype(F32)).astype(BF16)
        return carry

    lax.fori_loop(0, 16, add_block, 0)
    blocks.begin()

    def hidden_one(t, carry):
        columns = pl.ds(pl.multiple_of(t * 256, 256), 256)
        weight = wrel[:, :, :, :, columns].reshape(NX * CL, 256)
        hid[:, :, columns] = dot(delta[...], weight, ((1,), (0,))).reshape(NZ, DOC, 256)
        return carry

    def combine(i, cols=slice(0, D), wait=True):
        t = (z + i) % NZ
        if wait:
            for copy in returns[i % NZ]:
                copy.wait_recv()
        hid[t, :, cols] = hid[t, :, cols] + dot(place[t], ret[t, :, cols], ((0,), (0,)))

    z_right, z_left = [None, None], [None, None]
    parts = (slice(0, D // 2), slice(D // 2, D))

    def z_send(h, p):
        z_right[p] = cp.start(zs_r.at[h - 1, p], zr_r.at[h - 1, p], me.at(dz=1))
        z_left[p] = cp.start(zs_l.at[h - 1, p], zr_l.at[h - 1, p], me.at(dz=-1))

    def z_step(h):
        right, left = (z + h) % NZ, (z - h) % NZ
        combine(h)
        combine(-h)
        for p, cols in enumerate(parts):
            z_right[p].wait_recv()
            z_left[p].wait_recv()
            if h == 3:
                zs_r[2, p, 0:half] = (hid[right, 0:half, cols] + zr_r[3, p, 0:half].astype(F32)).astype(BF16)
                zs_r[2, p, half:DOC] = hid[right, half:DOC, cols].astype(BF16)
                zs_l[2, p, half:DOC] = (hid[left, half:DOC, cols] + zr_l[3, p, half:DOC].astype(F32)).astype(BF16)
                zs_l[2, p, 0:half] = hid[left, 0:half, cols].astype(BF16)
            else:
                zs_r[h - 1, p] = (hid[right, :, cols] + zr_r[h, p].astype(F32)).astype(BF16)
                zs_l[h - 1, p] = (hid[left, :, cols] + zr_l[h, p].astype(F32)).astype(BF16)
            z_send(h, p)

    c_core = []

    def grad_of(g):
        lax.fori_loop(2 * g, 2 * g + 2, grad_one, 0)
        c_core.append(
            cp.start(gc.at[pl.ds(0, NY), 1 - c, g], c_in.at[pl.ds(0, NY), g], me.at(dc=1))
        )

    def add_cluster(i, carry):
        t, g = i // 4, i % 4
        gc[t, c, g] = (gc[t, c, g].astype(F32) + c_in[t, g].astype(F32)).astype(BF16)
        return carry

    def put(ref):
        def store(at, value):
            ref[at] = value.astype(ref.dtype)

        return store

    def put_b(at, value):
        o_c[pl.ds(64 + at.start, at.size)] = value

    for g in range(NX):
        grad_of(g)
    for copy in c_core:
        copy.wait_recv()
    lax.fori_loop(0, 16, add_cluster, 0)
    first_a.begin()
    first_b.begin()
    for p, cols in enumerate(parts):
        lax.fori_loop(2 * p, 2 * p + 2, hidden_one, 0)
        combine(4, cols, p == 0)
        zs_r[3, p, 0:half] = hid[opposite, 0:half, cols].astype(BF16)
        zs_l[3, p, half:DOC] = hid[opposite, half:DOC, cols].astype(BF16)
        z_right[p] = cp.start(zs_r.at[3, p, halves[0]], zr_r.at[3, p, halves[0]], me.at(dz=1))
        z_left[p] = cp.start(zs_l.at[3, p, halves[1]], zr_l.at[3, p, halves[1]], me.at(dz=-1))
    send_back(1)
    send_back(-1)
    first_a.middle()
    z_step(3)
    blocks.middle()
    first_b.middle()
    send_back(0)
    z_step(2)
    first_a.end(put(c_a))
    then_a.begin()
    z_step(1)
    then_a.middle()
    first_b.end(put(c_b))
    then_b.begin()
    blocks.end(put(o_b))
    done_b = pltpu.make_async_copy(o_b, out_b, local.at[7])
    done_b.start()
    combine(0)
    then_a.end(put(o_c))
    then_b.middle()
    for p, cols in enumerate(parts):
        z_right[p].wait_recv()
        z_left[p].wait_recv()
        o_h[:, cols] = (hid[z, :, cols] + zr_r[0, p].astype(F32) + zr_l[0, p].astype(F32)).astype(BF16)
    done_h = pltpu.make_async_copy(o_h, out_h, local.at[8])
    done_h.start()
    then_b.end(put_b)
    done_c = pltpu.make_async_copy(o_c, out_c, local.at[6])
    done_c.start()
    for copy in (done_c, done_b, done_h):
        copy.wait()
    cp.finish()


def w_part(wrel, group, y, c, part):
    return wrel.at[group, y, c, pl.ds(part * 32, 32)]


def per_device(encoded, positive_clusters, cluster_weight, shortlist, positive_offsets, block_weight):
    vmem = pl.BlockSpec(memory_space=pltpu.VMEM)
    hbm = pl.BlockSpec(memory_space=pl.ANY)
    bf = lambda *shape: pltpu.VMEM(shape, BF16)
    f32 = lambda *shape: pltpu.VMEM(shape, F32)
    copies = 128
    out_h, out_c, out_b = pl.pallas_call(
        kernel,
        out_shape=(
            jax.ShapeDtypeStruct((DOC, D), BF16),
            jax.ShapeDtypeStruct((128, CL), F32),
            jax.ShapeDtypeStruct((2048, 128), F32),
        ),
        in_specs=[hbm] * 6,
        out_specs=(hbm,) * 3,
        scratch_shapes=[
            bf(NZ, DOC, D), bf(D, NZ * DOC), bf(NX, NY, NC, 64, D), bf(16, LBL, D),
            pltpu.VMEM((NZ, 16, 128), jnp.int32), f32(NZ * DOC, 16), bf(NX, NZ, 32, D), f32(NX, NZ, 128),
            f32(16, 64), bf(NZ, 128, 128), bf(NZ, 128, D), bf(16, 64, D), bf(NZ * DOC, NX * CL),
            bf(NZ, 128, D), f32(NZ, DOC, D), bf(4, 2, DOC, D // 2), bf(4, 2, DOC, D // 2), bf(4, 2, DOC, D // 2),
            bf(4, 2, DOC, D // 2),
            bf(NY, NC, NX, 128, CL), bf(NY, NX, 128, CL),
            bf(4, 64, CL), bf(2, 4, 64, CL), bf(2, 4, 64, CL), bf(4, 64, CL), bf(2, 4, 64, CL), bf(2, 4, 64, CL),
            bf(4, 64, CL), bf(4, 64, CL), bf(64, CL), bf(2, 64, CL), bf(2, 64, CL), bf(64, CL), bf(2, 64, CL), bf(2, 64, CL),
            bf(NY, NC, 2048, 128), bf(NY, 2048, 128), bf(2048, 128), bf(2, 2048, 128), bf(2, 2048, 128),
            bf(DOC, D), f32(128, CL), f32(2048, 128),
            pltpu.SemaphoreType.DMA((copies,)),
            pltpu.SemaphoreType.DMA((copies,)),
            pltpu.SemaphoreType.DMA((9,)),
        ],
        compiler_params=pltpu.CompilerParams(
            collective_id=0, has_side_effects=True, vmem_limit_bytes=VMEM_LIMIT
        ),
    )(
        encoded, cluster_weight.reshape(NY, NC, 64, D), positive_clusters.T, shortlist.T,
        positive_offsets.T, block_weight,
    )
    out_h, out_c, out_b = pl.pallas_call(
        place_kernel,
        out_shape=(
            jax.ShapeDtypeStruct((DOC, D), BF16),
            jax.ShapeDtypeStruct((CL, 128), F32),
            jax.ShapeDtypeStruct((2048, 128), F32),
        ),
        in_specs=[vmem] * 3,
        out_specs=(vmem,) * 3,
    )(out_h, out_c, out_b)
    return out_h, out_c, out_b.reshape(16, LBL, 128)


def place_kernel(in_h, in_c, in_b, out_h, out_c, out_b):
    out_h[...] = in_h[...]
    out_c[...] = jnp.transpose(in_c[...], (1, 0))
    out_b[...] = in_b[...]


def solution(mesh):
    placed = (
        P(("dp", "label"), None),
        P(("dp", "label"), None),
        P("label", None),
        P(("dp", "label"), None),
        P(("dp", "label"), None),
        P("label", None, None),
    )
    return jax.shard_map(
        per_device,
        mesh=mesh,
        in_specs=placed,
        out_specs=(P(("dp", "label"), None), P("label", "dp"), P("label", None, "dp")),
        check_vma=False,
    )
```

```python
import math

import jax
import jax.numpy as jnp
from jax import lax
from jax.experimental import pallas as pl
from jax.experimental.pallas import tpu as pltpu
from jax.sharding import PartitionSpec as P

MESH = pl.DeviceIdType.MESH
F32, BF16 = jnp.float32, jnp.bfloat16
NY, NC, NX, NZ = 4, 2, 4, 8
DOC, D, CL, LBL = 128, 1024, 512, 128
VMEM_LIMIT = 60 * 1024 * 1024


class Spot:
    def __init__(self):
        dp, label = lax.axis_index("dp"), lax.axis_index("label")
        self.y, self.c = dp // NC, dp % NC
        self.x, self.z = label // NZ, label % NZ

    def at(self, dx=0, dy=0, dz=0, dc=0):
        y, x, z = (self.y + dy) % NY, (self.x + dx) % NX, (self.z + dz) % NZ
        return (y * NC + (self.c + dc) % NC, x * NZ + z)


class Copies:
    def __init__(self, send, recv):
        self.send, self.recv, self.used, self.sent = send, recv, 0, []

    def start(self, src, dst, device):
        i = self.used
        self.used += 1
        copy = pltpu.make_async_remote_copy(
            src_ref=src, dst_ref=dst, send_sem=self.send.at[i], recv_sem=self.recv.at[i],
            device_id=device, device_id_type=MESH,
        )
        copy.start()
        self.sent.append(copy)
        return copy

    def finish(self):
        for copy in self.sent:
            copy.wait_send()


class Chain:
    def __init__(self, cp, side, own, two, s, r, rows=0):
        self.cp, self.side, self.own, self.two, self.s, self.r, self.rows = cp, side, own, two, s, r, rows

    def piece(self, j):
        return pl.ds(j * self.rows, self.rows) if self.rows else j

    def pair(self, j):
        return pl.ds(j * (self.rows or 1), 2 * (self.rows or 1))

    def begin(self):
        a, b = self.pair(0), self.pair(2)
        self.moving = [
            self.cp.start(self.own(2, a), self.two.at[a], self.side(1)),
            self.cp.start(self.own(2, b), self.two.at[b], self.side(-1)),
        ]

    def arrive(self):
        for copy in self.moving:
            copy.wait_recv()

    def middle(self):
        self.arrive()
        for j in range(4):
            at = self.piece(j)
            self.s[j // 2, at] = (self.own(1 + j // 2 * 2, at)[...].astype(F32) + self.two[at].astype(F32)).astype(BF16)
            self.s[1 - j // 2, at] = self.own(3 - j // 2 * 2, at)[...]
        self.moving = [
            self.cp.start(self.s.at[0], self.r.at[0], self.side(1)),
            self.cp.start(self.s.at[1], self.r.at[1], self.side(-1)),
        ]

    def end(self, put):
        self.arrive()
        for j in range(4):
            at = self.piece(j)
            put(at, self.own(0, at)[...].astype(F32) + self.r[0, at].astype(F32) + self.r[1, at].astype(F32))


def dot(a, b, dims):
    return lax.dot_general(a, b, (dims, ((), ())), preferred_element_type=F32)


def sigmoid(v):
    return 0.5 * jnp.tanh(0.5 * v) + 0.5


def iota(shape, dim):
    return lax.broadcasted_iota(jnp.int32, shape, dim)


def kernel(
    enc, w, pos, listed, offsets, bw_hbm, out_h, out_c, out_b,
    docs, docs_t, wrel, bw, metas, pos_t, arr, tgt, off, place, disp, rows_p, delta,
    ret, hid, zs_r, zs_l, zr_r, zr_l,
    gc, c_in, fa_2, fa_s, fa_r, fb_2, fb_s, fb_r, c_a, c_b, ga_2, ga_s, ga_r, gb_2, gb_s, gb_r,
    gb, b_in, by_2, by_s, by_r, o_h, o_c, o_b, send, recv, local,
):
    me = Spot()
    x, y, z, c = me.x, me.y, me.z, me.c
    scale = 1.0 / math.sqrt(DOC * NY * NC * NX * NZ)
    own = [
        pltpu.make_async_copy(enc, docs.at[z], local.at[0]),
        pltpu.make_async_copy(pos, metas.at[z, pl.ds(0, 4)], local.at[1]),
        pltpu.make_async_copy(listed, metas.at[z, pl.ds(4, 4)], local.at[2]),
        pltpu.make_async_copy(offsets, metas.at[z, pl.ds(8, 4)], local.at[3]),
        pltpu.make_async_copy(w, wrel.at[0], local.at[4]),
        pltpu.make_async_copy(bw_hbm, bw, local.at[5]),
    ]
    for copy in own:
        copy.start()
    metas[z, 12:16] = jnp.zeros((4, 128), jnp.int32)
    others = (
        [me.at(dz=i) for i in range(1, NZ)] + [me.at(dx=i) for i in range(1, NX)]
        + [me.at(dy=1), me.at(dy=-1), me.at(dc=1)]
    )
    barrier = pltpu.get_barrier_semaphore()
    for other in others:
        pl.semaphore_signal(barrier, inc=1, device_id=other, device_id_type=MESH)
    cp = Copies(send, recv)
    half = DOC // 2

    slot = iota((128, 128), 0)
    lane = iota((128, 128), 1)
    block = (((x + (slot >> 5)) & 3) * NZ + z) * 16 + (slot & 15)
    turn = ((slot >> 4) & 1).astype(F32)
    upper = jnp.where(slot < lane, 1.0, 0.0).astype(BF16)
    eye = jnp.where(slot == lane, 1.0, 0.0).astype(BF16)
    row8 = iota((8, 128), 0)
    tgt[0] = jnp.zeros((8, 128), F32)
    arrivals = [[] for _ in range(NX)]

    def choose(zs):
        info = metas[zs]
        named = jnp.zeros((128, 128), F32)
        offset = jnp.zeros((128, 128), F32)
        for k in range(4):
            hit = info[4 + k:5 + k, :] == block
            named = jnp.where(hit, 1.0, named)
            offset = jnp.where(hit, (info[8 + k:9 + k, :] + 1).astype(F32), offset)
        rank = dot(named.astype(BF16), upper, ((1,), (0,)))
        chosen = jnp.where(rank == turn, named, 0.0)
        place[zs] = chosen.astype(BF16)
        disp[zs] = dot(chosen.astype(BF16), docs[zs], ((1,), (0,))).astype(BF16)
        pick = jnp.where(row8 == zs, 1.0, 0.0).astype(BF16)
        tgt[0] += dot(pick, (chosen * offset).astype(BF16), ((1,), (1,)))

    def hand_on(zs):
        for d in (2, 1, 3):
            arrivals[NX - d].append(
                cp.start(disp.at[zs, pl.ds(d * 32, 32)], arr.at[NX - d, zs], me.at(dx=d))
            )
        arr[0, zs] = disp[zs, 0:32]

    def dispatch(zs):
        choose(zs)
        hand_on(zs)

    def prepare(zs):
        columns = pl.ds(pl.multiple_of(zs * 128, 128), 128)
        for j in range(D // 128):
            docs_t[pl.ds(j * 128, 128), columns] = dot(
                eye, docs[zs, :, j * 128:(j + 1) * 128], ((1,), (1,))
            ).astype(BF16)
        pos_t[columns, :] = jnp.transpose(metas[zs].astype(F32), (1, 0))

    def first(tile, pos, base):
        ids = (base + iota((1, tile.shape[1]), 1)).astype(F32)
        hit = pos[:, 0:1] == ids
        for k in range(1, 4):
            hit = hit | (pos[:, k:k + 1] == ids)
        return (sigmoid(tile) - jnp.where(hit, 1.0, 0.0)).astype(BF16)

    def own_group(zs):
        rows = pl.ds(pl.multiple_of(zs * 128, 128), 128)
        tile = dot(docs[zs], wrel[0].reshape(CL, D), ((1,), (1,)))
        delta[rows, 0:CL] = first(tile, pos_t[rows, :], (x * NZ + z) * CL)

    for i in range(4):
        own[i].wait()
    choose(z)
    prepare(z)
    pl.semaphore_wait(barrier, len(others))
    halves = (pl.ds(0, half), pl.ds(half, half))

    def pass_on(zs, part, dz):
        return cp.start(docs.at[zs, halves[part]], docs.at[zs, halves[part]], me.at(dz=dz))

    right, left = [None, None], [None, None]
    for part in range(2):
        right[part] = pass_on(z, part, 1)
        left[1 - part] = pass_on(z, 1 - part, -1)
    w_right = cp.start(w.at[y, c], wrel.at[3, y, c], me.at(dx=1))
    w_left = cp.start(w.at[y, c], wrel.at[1, y, c], me.at(dx=-1))
    got_meta = [None] + [cp.start(metas.at[z], metas.at[z], me.at(dz=i)) for i in range(1, NZ)]
    own[4].wait()
    own_group(z)
    groups = pl.ds(1, 3)
    w_right.wait_recv()
    w_left.wait_recv()
    w_right = cp.start(w_part(wrel, 3, y, c, 0), w_part(wrel, 2, y, c, 0), me.at(dx=1))
    w_left = cp.start(w_part(wrel, 1, y, c, 1), w_part(wrel, 2, y, c, 1), me.at(dx=-1))
    hand_on(z)
    for h in range(1, NZ // 2):
        from_left, from_right = (z - h) % NZ, (z + h) % NZ
        for part in range(2):
            right[part].wait_recv()
            if h + 1 < NZ // 2 or part == 0:
                right[part] = pass_on(from_left, part, 1)
            left[1 - part].wait_recv()
            if h + 1 < NZ // 2 or part == 0:
                left[1 - part] = pass_on(from_right, 1 - part, -1)
        if h == 1:
            w_right.wait_recv()
            w_left.wait_recv()
            y_right = cp.start(wrel.at[groups, y, c], wrel.at[groups, y, c], me.at(dy=1))
            y_left = cp.start(wrel.at[groups, y, c], wrel.at[groups, y, c], me.at(dy=-1))
            sib = [cp.start(wrel.at[groups, y, c], wrel.at[groups, y, c], me.at(dc=1))]
        got_meta[h].wait_recv()
        dispatch(from_left)
        got_meta[NZ - h].wait_recv()
        dispatch(from_right)
        if h == 3:
            y_right.wait_recv()
            y_left.wait_recv()
            yl, yr = (y - 1) % NY, (y + 1) % NY
            a, b = pl.ds(0, 32), pl.ds(32, 32)
            y_right = cp.start(wrel.at[groups, yl, c, a], wrel.at[groups, yl, c, a], me.at(dy=1))
            y_left = cp.start(wrel.at[groups, yr, c, b], wrel.at[groups, yr, c, b], me.at(dy=-1))
            sib.append(cp.start(wrel.at[groups, yl, c], wrel.at[groups, yl, c], me.at(dc=1)))
            sib.append(cp.start(wrel.at[groups, yr, c], wrel.at[groups, yr, c], me.at(dc=1)))
        for zs in (from_left, from_right):
            prepare(zs)
            own_group(zs)
    right[0].wait_recv()
    left[1].wait_recv()
    got_meta[NZ // 2].wait_recv()
    opposite = (z + NZ // 2) % NZ
    dispatch(opposite)
    for d in range(1, NX):
        arrivals[NX - d].append(cp.start(tgt.at[0], tgt.at[NX - d], me.at(dx=d)))
    prepare(opposite)
    own_group(opposite)

    def scores_one(copies, yi):
        for copy in copies:
            copy.wait_recv()
        weight = wrel[1:NX, yi].reshape(3 * 128, D)
        tile = dot(docs[...].reshape(NZ * DOC, D), weight, ((1,), (1,)))
        for g in range(1, NX):
            base = (((x + g) % NX) * NZ + z) * CL + yi * 128
            columns = pl.ds(pl.multiple_of(g * CL + yi * 128, 128), 128)
            delta[:, columns] = first(tile[:, (g - 1) * 128:g * 128], pos_t[...], base)

    scores_one(sib[0:1], y)
    scores_one(sib[1:2], yl)
    y_right.wait_recv()
    y_left.wait_recv()
    far = (y + 2) % NY
    sib.append(cp.start(wrel.at[groups, far, c], wrel.at[groups, far, c], me.at(dc=1)))
    scores_one(sib[2:3], yr)

    to, fro = iota((256, 256), 0), iota((256, 256), 1)
    moved = ((to >> 1) & 7) * 32 + (to & 1) * 16 + (to >> 4)
    shuffle = jnp.where(fro == moved, 1.0, 0.0).astype(BF16)
    offs = jnp.zeros((16, 64), F32)
    for e in range(NX):
        for copy in arrivals[e]:
            copy.wait_recv()
        rows = dot(shuffle, arr[e].reshape(256, D), ((1,), (0,))).astype(BF16)
        rows_p[:, e * 16:(e + 1) * 16, :] = rows.reshape(16, 16, D)
        for t in range(2):
            at = ((NX - e) % NX) * 32 + t * 16
            take = jnp.where(iota((16, 128), 1) == iota((16, 128), 0) + at, 1.0, 0.0).astype(BF16)
            put = jnp.where(iota((8, 64), 1) == iota((8, 64), 0) * 2 + (e * 16 + t), 1.0, 0.0).astype(BF16)
            taken = dot(take, tgt[e].astype(BF16), ((1,), (1,))).astype(BF16)
            offs = offs + dot(taken, put, ((1,), (0,)))
    off[...] = offs
    own[5].wait()

    def second(i, carry):
        pair = (2 * i, 2 * i + 1)
        scores = [dot(bw[b], rows_p[b], ((1,), (1,))) for b in pair]
        dts = []
        for b, score in zip(pair, scores):
            wanted = off[pl.ds(b, 1), :]
            target = jnp.where(iota((LBL, 64), 0).astype(F32) + 1.0 == wanted, 1.0, 0.0)
            dts.append(jnp.where(wanted > 0.0, sigmoid(score) - target, 0.0).astype(BF16))
        grads = [dot(dt, rows_p[b], ((1,), (0,))) for b, dt in zip(pair, dts)]
        backs = [dot(dt, bw[b], ((0,), (0,))) for b, dt in zip(pair, dts)]
        for b, grad, value in zip(pair, grads, backs):
            at = pl.ds(pl.multiple_of(b * LBL, LBL), LBL)
            grad = (grad * scale).astype(BF16)
            for j in range(NY * NC):
                gb[j // NC, j % NC, at, :] = grad[:, j * 128:(j + 1) * 128]
            rows_p[b] = value.astype(BF16)
        return carry

    b_core = []
    for i in range(2):
        lax.fori_loop(4 * i, 4 * i + 4, second, 0)
        rows = pl.ds(1024 * i, 1024)
        b_core.append(
            cp.start(gb.at[pl.ds(0, NY), 1 - c, rows], b_in.at[pl.ds(0, NY), rows], me.at(dc=1))
        )
    for e in (2, 1, 3, 0):
        rows = dot(shuffle, rows_p[:, e * 16:(e + 1) * 16, :].reshape(256, D), ((0,), (0,)))
        arr[e] = rows.astype(BF16).reshape(NZ, 32, D)
    returns = [[] for _ in range(NZ)]

    def send_back(i):
        t = (z + i) % NZ
        for e in (2, 1, 3):
            dst = ret.at[t, pl.ds((NX - e) * 32, 32)]
            returns[i % NZ].append(cp.start(arr.at[e, t], dst, me.at(dx=e)))

    for i in (4, 3, -3, 2, -2):
        send_back(i)
    for i in range(NZ):
        ret[i, 0:32] = arr[0, i]

    def grad_one(t, carry):
        columns = pl.ds(pl.multiple_of(t * 256, 256), 256)
        grad = dot(docs_t[...], delta[:, columns], ((1,), (0,))) * scale
        at = pl.ds(pl.multiple_of((t % 2) * 256, 256), 256)
        gc[:, :, t // 2, :, at] = grad.astype(BF16).reshape(NY, NC, 128, 256)
        return carry

    along_x, along_y = (lambda i: me.at(dx=i)), (lambda i: me.at(dy=i))
    a_rows, b_rows = pl.ds(0, 64), pl.ds(64, 64)
    blocks = Chain(cp, along_y, lambda k, at: gb.at[(y + k) % NY, c, at], by_2, by_s, by_r, 512)
    first_a = Chain(cp, along_y, lambda k, at: gc.at[(y + k) % NY, c, at, a_rows], fa_2, fa_s, fa_r)
    first_b = Chain(cp, along_x, lambda k, at: gc.at[at, c, k, b_rows], fb_2, fb_s, fb_r)
    then_a = Chain(cp, along_x, lambda k, at: c_a.at[k, at], ga_2, ga_s, ga_r, 16)
    then_b = Chain(cp, along_y, lambda k, at: c_b.at[(y + k) % NY, at], gb_2, gb_s, gb_r, 16)

    scores_one(sib[3:4], far)
    for copy in b_core:
        copy.wait_recv()

    def add_block(i, carry):
        rows = pl.ds(pl.multiple_of((i % 4) * 512, 512), 512)
        gb[i // 4, c, rows] = (gb[i // 4, c, rows].astype(F32) + b_in[i // 4, rows].astype(F32)).astype(BF16)
        return carry

    lax.fori_loop(0, 16, add_block, 0)
    blocks.begin()

    def hidden_one(t, carry):
        columns = pl.ds(pl.multiple_of(t * 256, 256), 256)
        weight = wrel[:, :, :, :, columns].reshape(NX * CL, 256)
        hid[:, :, columns] = dot(delta[...], weight, ((1,), (0,))).reshape(NZ, DOC, 256)
        return carry

    def combine(i, cols=slice(0, D), wait=True):
        t = (z + i) % NZ
        if wait:
            for copy in returns[i % NZ]:
                copy.wait_recv()
        hid[t, :, cols] = hid[t, :, cols] + dot(place[t], ret[t, :, cols], ((0,), (0,)))

    z_right, z_left = [None, None], [None, None]
    parts = (slice(0, D // 2), slice(D // 2, D))

    def z_send(h, p):
        z_right[p] = cp.start(zs_r.at[h - 1, p], zr_r.at[h - 1, p], me.at(dz=1))
        z_left[p] = cp.start(zs_l.at[h - 1, p], zr_l.at[h - 1, p], me.at(dz=-1))

    def z_step(h):
        right, left = (z + h) % NZ, (z - h) % NZ
        combine(h)
        combine(-h)
        for p, cols in enumerate(parts):
            z_right[p].wait_recv()
            z_left[p].wait_recv()
            if h == 3:
                zs_r[2, p, 0:half] = (hid[right, 0:half, cols] + zr_r[3, p, 0:half].astype(F32)).astype(BF16)
                zs_r[2, p, half:DOC] = hid[right, half:DOC, cols].astype(BF16)
                zs_l[2, p, half:DOC] = (hid[left, half:DOC, cols] + zr_l[3, p, half:DOC].astype(F32)).astype(BF16)
                zs_l[2, p, 0:half] = hid[left, 0:half, cols].astype(BF16)
            else:
                zs_r[h - 1, p] = (hid[right, :, cols] + zr_r[h, p].astype(F32)).astype(BF16)
                zs_l[h - 1, p] = (hid[left, :, cols] + zr_l[h, p].astype(F32)).astype(BF16)
            z_send(h, p)

    c_core = []

    def grad_of(g):
        lax.fori_loop(2 * g, 2 * g + 2, grad_one, 0)
        c_core.append(
            cp.start(gc.at[pl.ds(0, NY), 1 - c, g], c_in.at[pl.ds(0, NY), g], me.at(dc=1))
        )

    def add_cluster(i, carry):
        t, g = i // 4, i % 4
        gc[t, c, g] = (gc[t, c, g].astype(F32) + c_in[t, g].astype(F32)).astype(BF16)
        return carry

    def put(ref):
        def store(at, value):
            ref[at] = value.astype(ref.dtype)

        return store

    def put_b(at, value):
        o_c[pl.ds(64 + at.start, at.size)] = value

    for g in range(NX):
        grad_of(g)
    for copy in c_core:
        copy.wait_recv()
    lax.fori_loop(0, 16, add_cluster, 0)
    first_a.begin()
    first_b.begin()
    for p, cols in enumerate(parts):
        lax.fori_loop(2 * p, 2 * p + 2, hidden_one, 0)
        combine(4, cols, p == 0)
        zs_r[3, p, 0:half] = hid[opposite, 0:half, cols].astype(BF16)
        zs_l[3, p, half:DOC] = hid[opposite, half:DOC, cols].astype(BF16)
        z_right[p] = cp.start(zs_r.at[3, p, halves[0]], zr_r.at[3, p, halves[0]], me.at(dz=1))
        z_left[p] = cp.start(zs_l.at[3, p, halves[1]], zr_l.at[3, p, halves[1]], me.at(dz=-1))
    send_back(1)
    send_back(-1)
    first_a.middle()
    z_step(3)
    blocks.middle()
    first_b.middle()
    send_back(0)
    z_step(2)
    first_a.end(put(c_a))
    then_a.begin()
    z_step(1)
    first_b.end(put(c_b))
    then_b.begin()
    then_a.middle()
    combine(0)
    then_b.middle()
    for p, cols in enumerate(parts):
        z_right[p].wait_recv()
        z_left[p].wait_recv()
        o_h[:, cols] = (hid[z, :, cols] + zr_r[0, p].astype(F32) + zr_l[0, p].astype(F32)).astype(BF16)
    done_h = pltpu.make_async_copy(o_h, out_h, local.at[8])
    done_h.start()
    then_a.end(put(o_c))
    blocks.end(put(o_b))
    done_b = pltpu.make_async_copy(o_b, out_b, local.at[7])
    done_b.start()
    then_b.end(put_b)
    done_c = pltpu.make_async_copy(o_c, out_c, local.at[6])
    done_c.start()
    for copy in (done_c, done_b, done_h):
        copy.wait()
    cp.finish()


def w_part(wrel, group, y, c, part):
    return wrel.at[group, y, c, pl.ds(part * 32, 32)]


def per_device(encoded, positive_clusters, cluster_weight, shortlist, positive_offsets, block_weight):
    vmem = pl.BlockSpec(memory_space=pltpu.VMEM)
    hbm = pl.BlockSpec(memory_space=pl.ANY)
    bf = lambda *shape: pltpu.VMEM(shape, BF16)
    f32 = lambda *shape: pltpu.VMEM(shape, F32)
    copies = 128
    out_h, out_c, out_b = pl.pallas_call(
        kernel,
        out_shape=(
            jax.ShapeDtypeStruct((DOC, D), BF16),
            jax.ShapeDtypeStruct((128, CL), F32),
            jax.ShapeDtypeStruct((2048, 128), F32),
        ),
        in_specs=[hbm] * 6,
        out_specs=(hbm,) * 3,
        scratch_shapes=[
            bf(NZ, DOC, D), bf(D, NZ * DOC), bf(NX, NY, NC, 64, D), bf(16, LBL, D),
            pltpu.VMEM((NZ, 16, 128), jnp.int32), f32(NZ * DOC, 16), bf(NX, NZ, 32, D), f32(NX, NZ, 128),
            f32(16, 64), bf(NZ, 128, 128), bf(NZ, 128, D), bf(16, 64, D), bf(NZ * DOC, NX * CL),
            bf(NZ, 128, D), f32(NZ, DOC, D), bf(4, 2, DOC, D // 2), bf(4, 2, DOC, D // 2), bf(4, 2, DOC, D // 2),
            bf(4, 2, DOC, D // 2),
            bf(NY, NC, NX, 128, CL), bf(NY, NX, 128, CL),
            bf(4, 64, CL), bf(2, 4, 64, CL), bf(2, 4, 64, CL), bf(4, 64, CL), bf(2, 4, 64, CL), bf(2, 4, 64, CL),
            bf(4, 64, CL), bf(4, 64, CL), bf(64, CL), bf(2, 64, CL), bf(2, 64, CL), bf(64, CL), bf(2, 64, CL), bf(2, 64, CL),
            bf(NY, NC, 2048, 128), bf(NY, 2048, 128), bf(2048, 128), bf(2, 2048, 128), bf(2, 2048, 128),
            bf(DOC, D), f32(128, CL), f32(2048, 128),
            pltpu.SemaphoreType.DMA((copies,)),
            pltpu.SemaphoreType.DMA((copies,)),
            pltpu.SemaphoreType.DMA((9,)),
        ],
        compiler_params=pltpu.CompilerParams(
            collective_id=0, has_side_effects=True, vmem_limit_bytes=VMEM_LIMIT
        ),
    )(
        encoded, cluster_weight.reshape(NY, NC, 64, D), positive_clusters.T, shortlist.T,
        positive_offsets.T, block_weight,
    )
    out_h, out_c, out_b = pl.pallas_call(
        place_kernel,
        out_shape=(
            jax.ShapeDtypeStruct((DOC, D), BF16),
            jax.ShapeDtypeStruct((CL, 128), F32),
            jax.ShapeDtypeStruct((2048, 128), F32),
        ),
        in_specs=[vmem] * 3,
        out_specs=(vmem,) * 3,
    )(out_h, out_c, out_b)
    return out_h, out_c, out_b.reshape(16, LBL, 128)


def place_kernel(in_h, in_c, in_b, out_h, out_c, out_b):
    out_h[...] = in_h[...]
    out_c[...] = jnp.transpose(in_c[...], (1, 0))
    out_b[...] = in_b[...]


def solution(mesh):
    placed = (
        P(("dp", "label"), None),
        P(("dp", "label"), None),
        P("label", None),
        P(("dp", "label"), None),
        P(("dp", "label"), None),
        P("label", None, None),
    )
    return jax.shard_map(
        per_device,
        mesh=mesh,
        in_specs=placed,
        out_specs=(P(("dp", "label"), None), P("label", "dp"), P("label", None, "dp")),
        check_vma=False,
    )
```
